256 devices in a mesh: dp: 32 (over z, x), seq: 8 (over y, core).
Axes of the slice: x: 4, y: 4, z: 8, core: 2. Of those that a mesh axis runs over, the one named last changes fastest.
Arguments:
- patches: bfloat16 [32, 98304], P(None, ('dp', 'seq')), may hold values from -12 to 12
- segment_ids: int32 [32, 3072], P('dp'), may hold values from 0 to 15, never falling along the last dimension, each value on 1 to 2304 neighbouring positions
- regroup_plan: int32 [32, 5, 64], P('dp'), may hold values from 0 to 383, as said below
- input_weight: bfloat16 [32, 1280], replicated, may hold values from -1 to 1
- input_bias: float32 [1280], replicated, may hold values from -3 to 3
- skip_weight: bfloat16 [32, 1280], replicated, may hold values from -1 to 1
- hidden_weight: bfloat16 [1280, 1280], replicated, may hold values from -0.15625 to 0.15625
- output_bias: float32 [1280], replicated, may hold values from -3 to 3
- norm_gain: float32 [1280], replicated, may hold values from 0.1 to 1.9
- head_scale: float32 [8], replicated, may hold values from 1 to 4
- qkv_weight: bfloat16 [1280, 3, 640], replicated, may hold values from -0.15625 to 0.15625
- out_weight: bfloat16 [640, 1280], P(None, ('dp', 'seq')), may hold values from -0.25 to 0.25
- cotangent: bfloat16 [98304, 1280], P(('dp', 'seq')), may hold values from -0.3125 to 0.3125
Outputs:
- layer_out: bfloat16 [98304, 1280], P(('dp', 'seq'))
- out_grad: float32 [640, 1280], P(None, ('dp', 'seq'))
The draws below stay inside these ranges and needn't reach their ends.
Inputs may be any that keep to these rules, and one draw needn't show every extreme that they name: `regroup_plan`: piece s * 8 + d of a window moves rows of source shard s to destination shard d: one piece for each pair, each moving one row or more. The pieces of a window cover each of the 384 rows of every source shard once and each of the 384 rows of every destination shard once. A piece moves at most 96 rows, and in every window some piece moves exactly 96. `segment_ids`: series ids never fall along a window's positions; one series of each window has exactly 2304 positions.
All inputs are finite; a program needn't handle non-finite values.
Results may differ from the reference program's by a relative error of at most 0.015.
Values may be sent and summed in bfloat16 or wider, within the bound.
A program may use at most 64 MiB of HBM per device.

```python
import math
import jax
import jax.numpy as jnp
import numpy as np
from jax import lax

D = 1280
FF = 1280
PATCH = 32
HD = 80
HEADS = 8
HW = 640
ROWS_DEV = 384
SEGS = 16
SHARDS = 8
WINDOW_LEN = 3072
MOST = 2304
WINDOWS = 32
TOKENS = 98304


def random_order(sub_key):
    return jax.random.permutation(sub_key, SHARDS)


def window_pieces(seed_key):
    shard_count = SHARDS
    unit_rows = ROWS_DEV // SHARDS
    first_key, second_key, third_key, fourth_key, fifth_key = jax.random.split(seed_key, 5)
    chosen = jax.random.permutation(first_key, shard_count)
    moved = jax.random.randint(second_key, (), 1, unit_rows)
    shares = jnp.full((shard_count,), unit_rows, jnp.int32)
    shares = shares.at[chosen[0]].add(unit_rows).at[chosen[1]].add(-moved).at[chosen[2]].add(moved - unit_rows)
    taker_perm = jax.random.permutation(fifth_key, shard_count)
    sender = jnp.broadcast_to(jnp.arange(shard_count, dtype=jnp.int32)[:, None], (shard_count, shard_count))
    taker = jnp.broadcast_to(jnp.arange(shard_count, dtype=jnp.int32)[None, :], (shard_count, shard_count))
    counts = shares[(taker_perm[taker] - sender) % shard_count]
    send_rank = jnp.argsort(jax.vmap(random_order)(jax.random.split(third_key, shard_count)), axis=1)
    first_rows = jnp.sum(jnp.where(send_rank[:, None, :] < send_rank[:, :, None], counts[:, None, :], 0), axis=2)
    take_rank = jnp.argsort(jax.vmap(random_order)(jax.random.split(fourth_key, shard_count)), axis=1)
    by_taker = jnp.transpose(counts)
    offsets = jnp.transpose(jnp.sum(jnp.where(take_rank[:, None, :] < take_rank[:, :, None], by_taker[:, None, :], 0), axis=2))
    fields = jnp.stack([sender, first_rows, counts, taker, offsets])
    return fields.reshape(5, shard_count * shard_count).astype(jnp.int32)


def draw_regroup_plan(key, part):
    return jax.vmap(window_pieces)(jax.random.split(jax.random.fold_in(key, 11), WINDOWS))


def draw_patches(key, part):
    scale_key, value_key = jax.random.split(jax.random.fold_in(key, 7))
    scales = jnp.exp(jax.random.uniform(scale_key, (1, TOKENS), jnp.float32, math.log(0.3), math.log(3.0)))
    raw_values = jnp.clip(jax.random.normal(value_key, (PATCH, TOKENS), jnp.float32), -4.0, 4.0)
    return (raw_values * scales).astype(jnp.bfloat16)


def spiked(result, own_key, source, target, parts, factor):
    def block_of(dim):
        return (jnp.arange(result.shape[dim]) // (result.shape[dim] // parts)).reshape((-1,) + (1,) * (result.ndim - 1 - dim))

    near = jax.random.permutation(own_key, parts)[block_of(target)]
    second = (block_of(target) + parts // 2) % parts
    return jnp.where((block_of(source) == near) | (block_of(source) == second), factor * result, result)


def levels(own_key, dims, cuts, least, high):
    level = 1.0
    for dim, blocks in cuts:
        draws = jax.random.uniform(jax.random.fold_in(jax.random.fold_in(own_key, 6), dim), (blocks,), jnp.float32, least / len(cuts), high / len(cuts))
        level = level * jnp.repeat(jnp.exp(draws), dims[dim] // blocks).reshape((-1,) + (1,) * (len(dims) - 1 - dim))
    return level


def split_up(count, total, limit, skew):
    portions = [(1 << 20) // math.isqrt(standing ** skew) + 1 for standing in range(2, count + 1)]
    spare, given = total - limit - (count - 1), [1] * (count - 1)
    while spare > 0:
        candidates = [i for i in range(count - 1) if given[i] < limit]
        whole, budget = sum([portions[i] for i in candidates]), spare
        for i in candidates:
            addition = min(limit - given[i], max(1, budget * portions[i] // whole), spare)
            given[i] = given[i] + addition
            spare = spare - addition
    return np.array([limit] + given)


def uneven_parts(key, number_of, total, bound, skew):
    if number_of == 2:
        one = jax.random.randint(key, (), max(1, total - bound), min(bound, total - 1) + 1)
        return jnp.stack([one, total - one])
    sizes = jnp.asarray(split_up(number_of, total, bound, skew), jnp.int32)
    twos = (number_of - 1) // 2
    source_of, sink = sizes[1:1 + 2 * twos:2], sizes[2:2 + 2 * twos:2]
    room = jnp.minimum(source_of - 1, bound - sink)
    passed = jax.random.randint(jax.random.fold_in(key, 1), (twos,), 0, 1 << 20) % (room + 1)
    sizes = sizes.at[1:1 + 2 * twos:2].set(source_of - passed).at[2:2 + 2 * twos:2].set(sink + passed)
    return sizes[jax.random.permutation(jax.random.fold_in(key, 2), number_of)]


def bell_draw(key, extent, deviation, most, shards=(), kind=jnp.bfloat16):
    entries = jax.random.normal(key, extent, jnp.float32) * deviation
    if len(shards) > 0:
        entries = levels(key, extent, shards, -0.22, 0.18) * entries
    return jnp.clip(entries, min=-most, max=most).astype(kind)


def heavy_noise(own_key, shape, scale, reach, shards, heavy, kind=jnp.bfloat16):
    result = scale * jax.random.normal(own_key, shape, jnp.float32)
    if shards:
        result = result * levels(own_key, shape, shards, -0.22, 0.18)
    return jnp.clip(spiked(result, jax.random.fold_in(own_key, 3), *heavy), -reach, reach).astype(kind)


def setup_inputs(seed: int = 0) -> dict:
    key_list = jax.random.split(jax.random.key(seed), 14)
    return {
        "patches": draw_patches(jax.random.fold_in(key_list[13], 71), 0),
        "segment_ids": jax.vmap(lambda own: jnp.searchsorted(jnp.cumsum(uneven_parts(own, SEGS, WINDOW_LEN, MOST, 2)), jnp.arange(WINDOW_LEN), side="right"))(jax.random.split(key_list[1], WINDOWS)).reshape((WINDOWS, WINDOW_LEN)).astype(jnp.int32),
        "regroup_plan": draw_regroup_plan(jax.random.fold_in(key_list[13], 71), 0),
        "input_weight": bell_draw(key_list[3], (PATCH, FF), PATCH ** -0.5, 1.0),
        "input_bias": bell_draw(key_list[4], (FF,), 0.5, 3.0, (), jnp.float32),
        "skip_weight": bell_draw(key_list[5], (PATCH, D), PATCH ** -0.5, 1.0),
        "hidden_weight": bell_draw(key_list[6], (FF, D), FF ** -0.5, 0.15625),
        "output_bias": bell_draw(key_list[7], (D,), 0.5, 3.0, (), jnp.float32),
        "norm_gain": jnp.clip(1.0 + 0.18 * jax.random.normal(key_list[8], (D,), jnp.float32), 0.1, 1.9),
        "head_scale": jnp.clip(jnp.exp(jax.random.uniform(key_list[9], (HEADS,), jnp.float32, math.log(1.0), math.log(4.0))), 1.0, 4.0),
        "qkv_weight": bell_draw(key_list[10], (D, 3, HW), D ** -0.5, 0.15625),
        "out_weight": bell_draw(key_list[11], (HW, D), HW ** -0.5, 0.25, ((1, 256),)),
        "cotangent": heavy_noise(key_list[12], (TOKENS, D), (4.0 * TOKENS ** -0.5), 0.3125, ((0, 256),), (0, 1, 256, 6.0)),
    }


EPSILON = 1e-06
CONTRACT_FIRST = (((0,), (0,)), ((), ()))

def row_norm(values):
    return values * lax.rsqrt(lax.optimization_barrier(jnp.mean(values * values, axis=-1, keepdims=True)) + EPSILON)

def round_half(values):
    return lax.optimization_barrier(values.astype(jnp.bfloat16)).astype(jnp.float32)

def place_table(plan_rows, shard_rows, shard_count):
    source = plan_rows[0]
    first_row = plan_rows[1]
    row_count = plan_rows[2]
    target = plan_rows[3]
    offset_row = plan_rows[4]
    window_len = shard_rows * shard_count
    loader_row = jnp.arange(window_len, dtype=jnp.int32)
    begin_row = source * shard_rows + first_row
    inside = (loader_row[None, :] >= begin_row[:, None]) & (loader_row[None, :] < (begin_row + row_count)[:, None])
    earlier = (source[:, None] == source[None, :]) & (target[:, None] == target[None, :]) & (first_row[None, :] < first_row[:, None])
    base_rank = lax.optimization_barrier(jnp.sum(jnp.where(earlier, row_count[None, :], 0), axis=1)).astype(jnp.int32)
    position = lax.optimization_barrier(jnp.sum(jnp.where(inside, (target * shard_rows + offset_row - begin_row)[:, None] + loader_row[None, :], 0), axis=0))
    slot_rank = lax.optimization_barrier(jnp.sum(jnp.where(inside, (base_rank - begin_row)[:, None] + loader_row[None, :], 0), axis=0))
    return (position.astype(jnp.int32), slot_rank.astype(jnp.int32))

def patch_block(columns, input_weight, input_bias, skip_weight, hidden_weight, output_bias):
    pre_act = lax.dot_general(columns, input_weight, CONTRACT_FIRST, preferred_element_type=jnp.float32) + input_bias
    hidden = jax.nn.silu(pre_act).astype(jnp.bfloat16)
    skipped = lax.dot_general(columns, skip_weight, CONTRACT_FIRST, preferred_element_type=jnp.float32)
    embedded = jnp.dot(hidden, hidden_weight, preferred_element_type=jnp.float32) + skipped + output_bias
    return embedded.astype(jnp.bfloat16)

def window_attention(projected, segment_row, head_scale):
    queries = round_half(row_norm(projected[:, 0].astype(jnp.float32)))
    key_rows = round_half(row_norm(projected[:, 1].astype(jnp.float32)))
    value_rows = projected[:, 2].astype(jnp.float32)
    block_len = min(512, WINDOW_LEN)
    position = jnp.arange(WINDOW_LEN, dtype=jnp.int32)
    factor = head_scale * (1.0 / math.sqrt(HD))

    def one_block(block_index):
        query_first = block_index * block_len
        query_part = lax.dynamic_slice_in_dim(queries, query_first, block_len, 0)
        scores = jnp.einsum('qhd,khd->hqk', query_part, key_rows) * factor[:, None, None]
        query_pos = query_first + jnp.arange(block_len, dtype=jnp.int32)
        query_seg = lax.dynamic_slice_in_dim(segment_row, query_first, block_len, 0)
        allowed = (query_seg[:, None] == segment_row[None, :]) & (position[None, :] <= query_pos[:, None])
        weights = jnp.where(allowed[None], jnp.exp(scores), 0.0)
        denominator = lax.optimization_barrier(jnp.sum(weights, axis=-1))
        summed = jnp.einsum('hqk,khd->qhd', round_half(weights), value_rows)
        return summed / jnp.transpose(denominator)[:, :, None]
    blocks = lax.map(one_block, jnp.arange(WINDOW_LEN // block_len, dtype=jnp.int32))
    return blocks.reshape(WINDOW_LEN, HW).astype(jnp.bfloat16)

def reference(patches, segment_ids, regroup_plan, input_weight, input_bias, skip_weight, hidden_weight, output_bias, norm_gain, head_scale, qkv_weight, out_weight, cotangent):

    def one_window(grad_sum, window_index):
        first_col = (window_index * WINDOW_LEN).astype(jnp.int32)
        columns = lax.dynamic_slice_in_dim(patches, first_col, WINDOW_LEN, 1)
        embedded = lax.optimization_barrier(patch_block(columns, input_weight, input_bias, skip_weight, hidden_weight, output_bias))
        plan_fields = lax.dynamic_index_in_dim(regroup_plan, window_index, 0, keepdims=False)
        position, slot_rank = place_table(plan_fields, ROWS_DEV, SHARDS)
        inverse = jnp.zeros((WINDOW_LEN,), jnp.int32).at[position].set(jnp.arange(WINDOW_LEN, dtype=jnp.int32))
        ordered = embedded[inverse]
        normed = (row_norm(ordered.astype(jnp.float32)) * norm_gain).astype(jnp.bfloat16)
        projected = jnp.dot(normed, qkv_weight.reshape(D, 3 * HW), preferred_element_type=jnp.float32)
        projected = lax.optimization_barrier(projected.astype(jnp.bfloat16)).reshape(WINDOW_LEN, 3, HEADS, HD)
        segment_row = lax.dynamic_index_in_dim(segment_ids, window_index, 0, keepdims=False)
        attended = window_attention(projected, segment_row, head_scale)
        layer_rows = (ordered.astype(jnp.float32) + jnp.dot(attended, out_weight, preferred_element_type=jnp.float32)).astype(jnp.bfloat16)
        grad_rows = lax.dynamic_slice_in_dim(cotangent, first_col, WINDOW_LEN, 0)
        grad_term = lax.dot_general(attended, grad_rows, CONTRACT_FIRST, preferred_element_type=jnp.float32)
        return (grad_sum + grad_term, layer_rows)
    grad_sum, layer_rows = lax.scan(one_window, jnp.zeros((HW, D), jnp.float32), jnp.arange(WINDOWS, dtype=jnp.int32))
    return (layer_rows.reshape(TOKENS, D), grad_sum)
```

```python
import functools
import math

import jax
import jax.numpy as jnp
from jax import lax
from jax.experimental import pallas as pl
from jax.experimental.pallas import tpu as pltpu
from jax.sharding import PartitionSpec as P

HD = 80
LANES = 128
ZN, XN, YN = 8, 4, 4
SEQ = 8
ROWS = 384
WIN = ROWS * SEQ
D = 1280
HW = 640
PATCH = 32
COLS = 5
GROUP = COLS * SEQ
EPS = 1e-06
MASKED = 2048.0
LOG2E = 1.4426950408889634
MESH = pl.DeviceIdType.MESH
BF = jnp.bfloat16
F32 = jnp.float32
NT = (((1,), (1,)), ((), ()))


def iota(shape, dim):
    return lax.broadcasted_iota(jnp.int32, shape, dim)


def dot(a, b):
    return jnp.dot(a, b, preferred_element_type=F32)


def dot_nt(a, b):
    return lax.dot_general(a, b, NT, preferred_element_type=F32)


def whole_layer(
    x_ref,
    seg_ref,
    plan_ref,
    win_ref,
    bin_ref,
    wskip_ref,
    wh_hbm,
    ob_ref,
    gain_ref,
    hs_ref,
    qkvw_hbm,
    ow_ref,
    cot_hbm,
    lo_ref,
    og_ref,
    wh,
    qkvw,
    cot,
    cot_t,
    xg,
    win8,
    wskip8,
    wsel,
    qkv,
    msend,
    emb_own,
    ow_send,
    w_land,
    wx,
    wt,
    att_send,
    ret,
    p_own,
    p_send,
    p_land,
    ya,
    ya_land,
    xb,
    xb_land,
    ax,
    ax_land,
    by,
    by_land,
    block40,
    fs,
    fs_land,
    ld_sem,
    x_s,
    x_r,
    w1_s,
    w1_r,
    w2_s,
    w2_r,
    w3_s,
    w3_r,
    w4_s,
    w4_r,
    m_s,
    m_r,
    a_s,
    a_r,
    p_s,
    p_r,
    ya_s,
    ya_r,
    xb_s,
    xb_r,
    ax_s,
    ax_r,
    by_s,
    by_r,
    f_s,
    f_r,
):
    dp = lax.axis_index("dp")
    s = lax.axis_index("seq")
    z = dp // XN
    xx = dp % XN
    y = s // 2
    c = s % 2
    mate = y * 2 + (1 - c)
    zmine = c * YN + y
    ownseq = (z % YN) * 2 + z // YN
    on_own = z == zmine

    def rcopy(src, dst, ssem, rsem, dp_t, seq_t):
        return pltpu.make_async_remote_copy(
            src_ref=src,
            dst_ref=dst,
            send_sem=ssem,
            recv_sem=rsem,
            device_id=(dp_t, seq_t),
            device_id_type=MESH,
        )

    def dpi(zz, x2):
        return zz * XN + x2

    loads = [
        pltpu.make_async_copy(qkvw_hbm, qkvw, ld_sem.at[0]),
        pltpu.make_async_copy(wh_hbm, wh, ld_sem.at[1]),
        pltpu.make_async_copy(cot_hbm, cot, ld_sem.at[2]),
    ]
    for ld in loads:
        ld.start()

    bar = pltpu.get_barrier_semaphore()

    def greet(dp_t, seq_t):
        pl.semaphore_signal(bar, inc=1, device_id=(dp_t, seq_t), device_id_type=MESH)

    for k in range(1, SEQ):
        greet(dp, (s + k) % SEQ)
    for k in range(1, XN):
        greet(dpi(z, (xx + k) % XN), s)
    for k in range(1, ZN):
        greet(dpi((z + k) % ZN, xx), ownseq)

    @pl.when(jnp.logical_not(on_own))
    def _():
        greet(dp, ownseq)

    for t in range(SEQ):

        @pl.when(jnp.logical_not(on_own & (s == t)))
        def _():
            greet(dpi(zmine, xx), jnp.int32(t))

    ow_send[...] = jnp.zeros((8, HW), F32)
    ow_send[0:COLS, :] = ow_ref[...].astype(F32)
    for k in range(SEQ):
        win8[k * PATCH : (k + 1) * PATCH, :] = win_ref[...]
        wskip8[k * PATCH : (k + 1) * PATCH, :] = wskip_ref[...]
    xg[pl.ds(pl.multiple_of(s * PATCH, PATCH), PATCH), :] = x_ref[...]

    pl.semaphore_wait(bar, 7 + 3 + 16 - 2 * on_own.astype(jnp.int32))

    def x_copy(k, source):
        rows = xg.at[pl.ds(pl.multiple_of(source * PATCH, PATCH), PATCH), :]
        return rcopy(x_ref, rows, x_s.at[k], x_r.at[k], dp, (s + k) % SEQ)

    for k in range(1, SEQ):
        x_copy(k, s).start()

    def w1_copy(k):
        return rcopy(
            ow_send, w_land.at[s], w1_s.at[k], w1_r.at[s], dpi((z + k) % ZN, xx), ownseq
        )

    for k in range(1, ZN):
        w1_copy(k).start()

    @pl.when(jnp.logical_not(on_own))
    def _():
        w1_copy(0).start()

    @pl.when(on_own)
    def _():
        w_land[s] = ow_send[...]

    loads[0].wait()
    feature = iota((HW, 2 * LANES), 0)
    lane2 = iota((HW, 2 * LANES), 1)
    inner = lane2 % LANES
    head = jnp.where(lane2 < LANES, s, mate)
    pick = jnp.where((inner < HD) & (feature == head * HD + inner), 1.0, 0.0).astype(BF)
    for i in range(3):

        def pick_rows(r, carry, i=i):
            rows = pl.ds(pl.multiple_of(r * 256, 256), 256)
            part = dot(qkvw[i, rows, :], pick).astype(BF)
            wsel[rows, i * LANES : (i + 1) * LANES] = part[:, :LANES]
            wsel[rows, (3 + i) * LANES : (4 + i) * LANES] = part[:, LANES:]
            return carry

        lax.fori_loop(0, D // 256, pick_rows, 0)

    loads[2].wait()
    for i in range(2):
        cot_t[i] = jnp.transpose(cot[:, i * HW : (i + 1) * HW])
    loads[1].wait()
    for k in range(1, SEQ):
        x_copy(k, (s - k + SEQ) % SEQ).wait_recv()

    def w2_copy(k, source):
        return rcopy(
            wx.at[xx] if source is None else wx.at[xx],
            wx.at[xx if source is None else source],
            w2_s.at[k],
            w2_r.at[k],
            dpi(z, (xx + k) % XN),
            s,
        )

    def wt_rows(zz):
        return wt.at[pl.ds(pl.multiple_of(zz * 160, 32), 160), :]

    def zof(seq):
        return (seq % 2) * YN + seq // 2

    def w3_copy(k, source):
        block = zof(s) if source is None else zof(source)
        return rcopy(
            wt_rows(zof(s)), wt_rows(block), w3_s.at[k], w3_r.at[k], dp, ((y + k) % YN) * 2 + c
        )

    def w4_copy(k, core):
        block = wt_rows(core * YN + (y - k + YN) % YN)
        return rcopy(block, block, w4_s.at[k], w4_r.at[k], dp, mate)

    def m_copy(i, core):
        rows = pl.multiple_of((2 * i + core) * ROWS, ROWS)
        return rcopy(msend.at[i], qkv.at[pl.ds(rows, ROWS), :], m_s.at[i], m_r.at[i], dp, mate)

    lane = iota((ROWS, LANES), 1)
    seg_lane = (lane >= HD) & (lane < HD + 16)

    def embed_chunk(i, carry):
        chunk = 2 * i + c
        first_row = pl.multiple_of(chunk * ROWS, ROWS)
        pos = first_row + iota((ROWS, 64), 0)
        source, first, count = plan_ref[0], plan_ref[1], plan_ref[2]
        start = plan_ref[3] * ROWS + plan_ref[4]
        inside = (pos >= start) & (pos < start + count)
        code = jnp.where(inside, (source * 512 + first - start) + pos, 0)
        code = jnp.sum(code.astype(F32), axis=1, keepdims=True).astype(jnp.int32)
        row_of = code % 512
        shard_of = code // 512
        onehot = jnp.where(iota((ROWS, ROWS), 1) == row_of, 1.0, 0.0).astype(BF)
        spread = dot_nt(onehot, xg[...])
        cols = jnp.where(
            iota((ROWS, SEQ * PATCH), 1) // PATCH == shard_of, spread, 0.0
        ).astype(BF)
        half = (dot(cols, win8[...]) + bin_ref[...]) * 0.5
        hidden = (half + half * jnp.tanh(half)).astype(BF)
        emb = (dot(hidden, wh[...]) + dot(cols, wskip8[...]) + ob_ref[...]).astype(BF)

        @pl.when(i == y)
        def _():
            emb_own[...] = emb

        wide = emb.astype(F32)
        scale = lax.rsqrt(jnp.mean(wide * wide, axis=-1, keepdims=True) + EPS)
        normed = (wide * scale * gain_ref[...]).astype(BF)
        proj = dot(normed, wsel[...]).astype(BF)

        seg_row = seg_ref[:, pl.ds(first_row, ROWS)]
        marks = jnp.where(iota((LANES, ROWS), 0) - HD == seg_row, 1.0, 0.0)
        marks = jnp.transpose(marks)
        away = jnp.where(seg_lane, (marks - 1.0) * MASKED, 0.0)
        ones = jnp.where(lane == HD, 1.0, 0.0)
        parts = []
        for h in range(2):
            q = proj[:, (3 * h) * LANES : (3 * h + 1) * LANES].astype(F32)
            k = proj[:, (3 * h + 1) * LANES : (3 * h + 2) * LANES].astype(F32)
            v = proj[:, (3 * h + 2) * LANES : (3 * h + 3) * LANES].astype(F32)
            q = q * lax.rsqrt(jnp.sum(q * q, axis=-1, keepdims=True) * (1.0 / HD) + EPS)
            k = k * lax.rsqrt(jnp.sum(k * k, axis=-1, keepdims=True) * (1.0 / HD) + EPS)
            parts.append([(q + away).astype(BF), (k + marks).astype(BF), (v + ones).astype(BF)])
        for j in range(3):
            msend[i, :, j * LANES : (j + 1) * LANES] = parts[1][j]
        m_copy(i, c).start()
        for j in range(3):
            qkv[pl.ds(first_row, ROWS), j * LANES : (j + 1) * LANES] = parts[0][j]

        @pl.when(i == 0)
        def _():
            for t in range(SEQ):

                @pl.when(jnp.logical_not(on_own & (s == t)))
                def _():
                    rcopy(ow_send, w_land.at[t], w1_s.at[0], w1_r.at[t], dp, mate).wait_recv()

            block = jnp.concatenate([w_land[t, 0:COLS, :] for t in range(SEQ)], axis=0)
            block = jnp.concatenate([block, jnp.zeros((8, HW), F32)], axis=0)
            wx[xx] = block.astype(BF)
            for k in range(1, XN):
                w2_copy(k, None).start()

        @pl.when(i == 1)
        def _():
            for k in range(1, XN):
                w2_copy(k, (xx - k + XN) % XN).wait_recv()
            block = jnp.concatenate([wx[j, 0:GROUP, :].astype(F32) for j in range(XN)], axis=0)
            wt[pl.ds(pl.multiple_of(zmine * 160, 32), 160), :] = block.astype(BF)
            for k in range(1, YN):
                w3_copy(k, None).start()
            w4_copy(0, c).start()

        return carry

    lax.fori_loop(0, 4, embed_chunk, 0)

    for k in range(1, YN):
        w3_copy(k, ((y - k + YN) % YN) * 2 + c).wait_recv()
        w4_copy(k, c).start()
    for i in range(4):
        m_copy(i, 1 - c).wait_recv()

    factor = hs_ref[s] * (LOG2E / math.sqrt(HD))
    causal = iota((ROWS, ROWS), 0) >= iota((ROWS, ROWS), 1)

    def a_copy(block, source, k):
        rows = ret.at[pl.ds(pl.multiple_of(source * HD, 16), HD), :]
        return rcopy(att_send.at[block], rows, a_s.at[k], a_r.at[k], dp, (s + k) % SEQ)

    for b in reversed(range(SEQ)):
        q = qkv[b * ROWS : (b + 1) * ROWS, 0:LANES]
        total = jnp.zeros((ROWS, LANES), F32)
        edges = list(range(0, b * ROWS, 2 * ROWS)) + [b * ROWS]
        for lo, hi in zip(edges[:-1], edges[1:]):
            scores = dot_nt(q, qkv[lo:hi, LANES : 2 * LANES]) * factor
            total = total + dot(jnp.exp2(scores).astype(BF), qkv[lo:hi, 2 * LANES : 3 * LANES])
        lo, hi = b * ROWS, (b + 1) * ROWS
        scores = dot_nt(q, qkv[lo:hi, LANES : 2 * LANES]) * factor
        weights = jnp.where(causal, jnp.exp2(scores), 0.0).astype(BF)
        total = total + dot(weights, qkv[lo:hi, 2 * LANES : 3 * LANES])
        across = jnp.transpose(total)
        out = (across[0:HD, :] / across[HD : HD + 1, :]).astype(BF)
        att_send[b] = out

        @pl.when(s == b)
        def _():
            ret[pl.ds(pl.multiple_of(s * HD, 16), HD), :] = out

        @pl.when(s != b)
        def _():
            a_copy(b, s, (b - s + SEQ) % SEQ).start()

    for k in range(1, SEQ):
        a_copy(0, (s - k + SEQ) % SEQ, k).wait_recv()

    attended = ret[...]
    p_send[...] = dot_nt(cot_t[1 - c], attended)
    pair = rcopy(p_send, p_land, p_s.at[0], p_r.at[0], dp, mate)
    pair.start()
    p_own[...] = dot_nt(cot_t[c], attended)

    pair.wait_recv()
    summed = p_own[...] + p_land[...]
    p_own[...] = summed
    half_rows = summed.reshape(YN, XN, GROUP, HW)
    for j in range(YN):
        ya[j] = summed[j * 160 : (j + 1) * 160, 0:ROWS].astype(BF)
    pad = jnp.zeros((YN, 8, HW - ROWS), F32)
    for j in range(XN):
        xb[j] = jnp.concatenate([half_rows[:, j, :, ROWS:], pad], axis=1).astype(BF)

    def ya_copy(k):
        to = (y + k) % YN
        return rcopy(ya.at[to], ya_land.at[k], ya_s.at[k], ya_r.at[k], dp, to * 2 + c)

    def xb_copy(k):
        to = (xx + k) % XN
        return rcopy(xb.at[to], xb_land.at[k], xb_s.at[k], xb_r.at[k], dpi(z, to), s)

    for k in range(1, YN):
        ya_copy(k).start()
        xb_copy(k).start()

    for k in range(YN):
        w4_copy(k, 1 - c).wait_recv()
    rows = jnp.transpose(attended)
    for j in range(5):
        cols = slice(j * 256, (j + 1) * 256)
        branch = dot_nt(rows, wt[cols, :])
        lo_ref[:, cols] = (emb_own[:, cols].astype(F32) + branch).astype(BF)

    for k in range(1, YN):
        ya_copy(k).wait_recv()
    own = p_own[pl.ds(pl.multiple_of(y * 160, 32), 160), :]
    a_sum = own[:, 0:ROWS]
    for k in range(1, YN):
        a_sum = a_sum + ya_land[k].astype(F32)
    pad = jnp.zeros((8, ROWS), F32)
    block40[...] = jnp.zeros_like(block40)
    for j in range(XN):
        piece = a_sum[j * GROUP : (j + 1) * GROUP, :]
        ax[j] = jnp.concatenate([piece, pad], axis=0).astype(BF)

        @pl.when(xx == j)
        def _():
            block40[:, 0:ROWS] = piece

    def ax_copy(k):
        to = (xx + k) % XN
        return rcopy(ax.at[to], ax_land.at[k], ax_s.at[k], ax_r.at[k], dpi(z, to), s)

    for k in range(1, XN):
        ax_copy(k).start()

    for k in range(1, XN):
        xb_copy(k).wait_recv()
    pad = jnp.zeros((8, HW - ROWS), F32)
    for j in range(YN):
        begin = pl.multiple_of((j * XN + xx) * GROUP, 8)
        piece = p_own[pl.ds(begin, GROUP), ROWS:HW]
        for k in range(1, XN):
            piece = piece + xb_land[k, j].astype(F32)[0:GROUP, :]
        by[j] = jnp.concatenate([piece, pad], axis=0).astype(BF)

        @pl.when(y == j)
        def _():
            block40[:, ROWS:HW] = piece

    def by_copy(k):
        to = (y + k) % YN
        return rcopy(by.at[to], by_land.at[k], by_s.at[k], by_r.at[k], dp, to * 2 + c)

    for k in range(1, YN):
        by_copy(k).start()
    for k in range(1, XN):
        ax_copy(k).wait_recv()
    for k in range(1, YN):
        by_copy(k).wait_recv()
    left = block40[:, 0:ROWS]
    right = block40[:, ROWS:HW]
    for k in range(1, XN):
        left = left + ax_land[k].astype(F32)[0:GROUP, :]
        right = right + by_land[k].astype(F32)[0:GROUP, :]
    block40[:, 0:ROWS] = left
    block40[:, ROWS:HW] = right
    fs[...] = jnp.zeros_like(fs)
    for t in range(SEQ):
        fs[t, 0:COLS, :] = block40[t * COLS : (t + 1) * COLS, :]

    def f_copy(t):
        return rcopy(fs.at[t], fs_land.at[z], f_s.at[t], f_r.at[z], dpi(zmine, xx), jnp.int32(t))

    for t in range(SEQ):

        @pl.when(jnp.logical_not(on_own & (s == t)))
        def _():
            f_copy(t).start()

        @pl.when(on_own & (s == t))
        def _():
            fs_land[z] = fs[t]

    for j in range(ZN):

        @pl.when(jnp.logical_not(on_own & (z == j)))
        def _():
            rcopy(fs.at[0], fs_land.at[j], f_s.at[0], f_r.at[j], dp, mate).wait_recv()

    final = fs_land[0]
    for j in range(1, ZN):
        final = final + fs_land[j]
    og_ref[...] = final[0:COLS, :]

    for k in range(1, SEQ):
        x_copy(k, s).wait_send()
        a_copy(0, s, k).wait_send()
    for k in range(1, ZN):
        w1_copy(k).wait_send()

    @pl.when(jnp.logical_not(on_own))
    def _():
        w1_copy(0).wait_send()

    for k in range(1, XN):
        w2_copy(k, None).wait_send()
        w3_copy(k, None).wait_send()
        ya_copy(k).wait_send()
        xb_copy(k).wait_send()
        ax_copy(k).wait_send()
        by_copy(k).wait_send()
    for k in range(YN):
        w4_copy(k, c).wait_send()
        m_copy(k, c).wait_send()
    pair.wait_send()
    for t in range(SEQ):

        @pl.when(jnp.logical_not(on_own & (s == t)))
        def _():
            f_copy(t).wait_send()


def per_device(
    patches,
    segment_ids,
    regroup_plan,
    input_weight,
    input_bias,
    skip_weight,
    hidden_weight,
    output_bias,
    norm_gain,
    head_scale,
    qkv_weight,
    out_weight,
    cotangent,
):
    vmem = pl.BlockSpec(memory_space=pltpu.VMEM)
    smem = pl.BlockSpec(memory_space=pltpu.SMEM)
    hbm = pl.BlockSpec(memory_space=pl.ANY)
    dma = pltpu.SemaphoreType.DMA
    scratch = [
        pltpu.VMEM((D, D), BF),
        pltpu.VMEM((3, D, HW), BF),
        pltpu.VMEM((ROWS, D), BF),
        pltpu.VMEM((2, HW, ROWS), BF),
        pltpu.VMEM((SEQ * PATCH, ROWS), BF),
        pltpu.VMEM((SEQ * PATCH, D), BF),
        pltpu.VMEM((SEQ * PATCH, D), BF),
        pltpu.VMEM((D, 6 * LANES), BF),
        pltpu.VMEM((WIN, 3 * LANES), BF),
        pltpu.VMEM((4, ROWS, 3 * LANES), BF),
        pltpu.VMEM((ROWS, D), BF),
        pltpu.VMEM((8, HW), F32),
        pltpu.VMEM((SEQ, 8, HW), F32),
        pltpu.VMEM((XN, 48, HW), BF),
        pltpu.VMEM((D, HW), BF),
        pltpu.VMEM((SEQ, HD, ROWS), BF),
        pltpu.VMEM((HW, ROWS), BF),
        pltpu.VMEM((HW, HW), F32),
        pltpu.VMEM((HW, HW), F32),
        pltpu.VMEM((HW, HW), F32),
        pltpu.VMEM((YN, 160, ROWS), BF),
        pltpu.VMEM((YN, 160, ROWS), BF),
        pltpu.VMEM((XN, YN, 48, HW - ROWS), BF),
        pltpu.VMEM((XN, YN, 48, HW - ROWS), BF),
        pltpu.VMEM((XN, 48, ROWS), BF),
        pltpu.VMEM((XN, 48, ROWS), BF),
        pltpu.VMEM((YN, 48, HW - ROWS), BF),
        pltpu.VMEM((YN, 48, HW - ROWS), BF),
        pltpu.VMEM((GROUP, HW), F32),
        pltpu.VMEM((SEQ, 8, HW), F32),
        pltpu.VMEM((ZN, 8, HW), F32),
        dma((3,)),
        dma((8,)),
        dma((8,)),
        dma((8,)),
        dma((8,)),
        dma((4,)),
        dma((4,)),
        dma((4,)),
        dma((4,)),
        dma((4,)),
        dma((4,)),
        dma((4,)),
        dma((4,)),
        dma((8,)),
        dma((8,)),
        dma((1,)),
        dma((1,)),
        dma((4,)),
        dma((4,)),
        dma((4,)),
        dma((4,)),
        dma((4,)),
        dma((4,)),
        dma((4,)),
        dma((4,)),
        dma((8,)),
        dma((8,)),
    ]
    layer_out, grad = pl.pallas_call(
        whole_layer,
        out_shape=(
            jax.ShapeDtypeStruct((ROWS, D), BF),
            jax.ShapeDtypeStruct((COLS, HW), F32),
        ),
        in_specs=[vmem, vmem, vmem, vmem, vmem, vmem, hbm, vmem, vmem, smem, hbm, vmem, hbm],
        out_specs=(vmem, vmem),
        scratch_shapes=scratch,
        compiler_params=pltpu.CompilerParams(
            collective_id=0, has_side_effects=True, vmem_limit_bytes=50 * 1024 * 1024
        ),
        name="whole_layer",
    )(
        patches,
        segment_ids,
        jnp.transpose(regroup_plan, (1, 0, 2)),
        input_weight,
        input_bias.reshape(1, -1),
        skip_weight,
        hidden_weight,
        output_bias.reshape(1, -1),
        norm_gain.reshape(1, -1),
        head_scale,
        jnp.transpose(qkv_weight, (1, 0, 2)),
        jnp.transpose(out_weight),
        cotangent,
    )
    return layer_out, jnp.transpose(grad)


def solution(mesh):
    placed = (
        P(None, ("dp", "seq")),
        P("dp", None),
        P("dp", None, None),
        P(),
        P(),
        P(),
        P(),
        P(),
        P(),
        P(),
        P(),
        P(None, ("dp", "seq")),
        P(("dp", "seq"), None),
    )
    return jax.shard_map(
        per_device,
        mesh=mesh,
        in_specs=placed,
        out_specs=(P(("dp", "seq"), None), P(None, ("dp", "seq"))),
        check_vma=False,
    )
```

```python
import functools
import math

import jax
import jax.numpy as jnp
from jax import lax
from jax.experimental import pallas as pl
from jax.experimental.pallas import tpu as pltpu
from jax.sharding import PartitionSpec as P

HD = 80
LANES = 128
ZN, XN, YN = 8, 4, 4
SEQ = 8
ROWS = 384
WIN = ROWS * SEQ
D = 1280
HW = 640
PATCH = 32
COLS = 5
GROUP = COLS * SEQ
EPS = 1e-06
MASKED = 2048.0
LOG2E = 1.4426950408889634
MESH = pl.DeviceIdType.MESH
BF = jnp.bfloat16
F32 = jnp.float32
NT = (((1,), (1,)), ((), ()))


def iota(shape, dim):
    return lax.broadcasted_iota(jnp.int32, shape, dim)


def dot(a, b):
    return jnp.dot(a, b, preferred_element_type=F32)


def dot_nt(a, b):
    return lax.dot_general(a, b, NT, preferred_element_type=F32)


def whole_layer(
    x_hbm,
    seg_hbm,
    plan_hbm,
    win_hbm,
    bin_hbm,
    wskip_hbm,
    wh_hbm,
    ob_hbm,
    gain_hbm,
    hs_hbm,
    qkvw_hbm,
    ow_hbm,
    cot_hbm,
    lo_ref,
    og_ref,
    x_ref,
    seg_ref,
    plan_ref,
    win_ref,
    bin_ref,
    wskip_ref,
    ob_ref,
    gain_ref,
    hs_ref,
    ow_ref,
    wh,
    qkvw,
    cot,
    cot_f,
    cot_t,
    xg,
    win8,
    wskip8,
    wsel,
    qkv,
    msend,
    emb_own,
    ow_send,
    w_land,
    wx,
    wt,
    wt_f,
    tiles,
    att_send,
    ret,
    p_own,
    p_send,
    p_land,
    ya,
    ya_land,
    xb,
    xb_land,
    ax,
    ax_land,
    by,
    by_land,
    block40,
    fs_f,
    fs,
    fs_land,
    ld_sem,
    x_s,
    x_r,
    w1_s,
    w1_r,
    w2_s,
    w2_r,
    w3_s,
    w3_r,
    w4_s,
    w4_r,
    m_s,
    m_r,
    a_s,
    a_r,
    p_s,
    p_r,
    ya_s,
    ya_r,
    xb_s,
    xb_r,
    ax_s,
    ax_r,
    by_s,
    by_r,
    f_s,
    f_r,
):
    dp = lax.axis_index("dp")
    s = lax.axis_index("seq")
    z = dp // XN
    xx = dp % XN
    y = s // 2
    c = s % 2
    mate = y * 2 + (1 - c)
    def rcopy(src, dst, ssem, rsem, dp_t, seq_t):
        return pltpu.make_async_remote_copy(
            src_ref=src,
            dst_ref=dst,
            send_sem=ssem,
            recv_sem=rsem,
            device_id=(dp_t, seq_t),
            device_id_type=MESH,
        )

    def dpi(zz, x2):
        return zz * XN + x2

    loads = [
        pltpu.make_async_copy(src, dst, ld_sem.at[i])
        for i, (src, dst) in enumerate(
            [
                (x_hbm, x_ref),
                (ow_hbm, ow_ref),
                (win_hbm, win_ref),
                (wskip_hbm, wskip_ref),
                (qkvw_hbm.at[:, :, pl.ds(pl.multiple_of(y * LANES, LANES), 2 * LANES)], qkvw),
                (plan_hbm, plan_ref),
                (seg_hbm, seg_ref),
                (bin_hbm, bin_ref),
                (ob_hbm, ob_ref),
                (gain_hbm, gain_ref),
                (hs_hbm, hs_ref),
                (wh_hbm, wh),
                (cot_hbm, cot),
            ]
        )
    ]
    for ld in loads:
        ld.start()

    bar = pltpu.get_barrier_semaphore()

    def greet(dp_t, seq_t):
        pl.semaphore_signal(bar, inc=1, device_id=(dp_t, seq_t), device_id_type=MESH)

    for k in range(1, SEQ):
        greet(dp, (s + k) % SEQ)
    for k in range(1, XN):
        greet(dpi(z, (xx + k) % XN), s)
    for k in range(1, ZN):
        greet(dpi((z + k) % ZN, xx), s)

    for ld in loads[:4]:
        ld.wait()
    ow_send[...] = jnp.zeros((8, HW), F32)
    ow_send[0:COLS, :] = ow_ref[...].astype(F32)
    for k in range(SEQ):
        win8[k * PATCH : (k + 1) * PATCH, :] = win_ref[...]
        wskip8[k * PATCH : (k + 1) * PATCH, :] = wskip_ref[...]
    xg[pl.ds(pl.multiple_of(s * PATCH, PATCH), PATCH), :] = x_ref[...]

    pl.semaphore_wait(bar, 7 + 3 + 7)

    def x_copy(k, source):
        rows = xg.at[pl.ds(pl.multiple_of(source * PATCH, PATCH), PATCH), :]
        return rcopy(x_ref, rows, x_s.at[k], x_r.at[k], dp, (s + k) % SEQ)

    for k in range(1, SEQ):
        x_copy(k, s).start()

    def w1_copy(k, source):
        slot = w_land.at[pl.ds(pl.multiple_of(source * 8, 8), 8), :]
        return rcopy(ow_send, slot, w1_s.at[k], w1_r.at[k], dpi((z + k) % ZN, xx), s)

    for k in range(1, ZN):
        w1_copy(k, z).start()
    w_land[pl.ds(pl.multiple_of(z * 8, 8), 8), :] = ow_send[...]

    loads[4].wait()
    feature = iota((2 * LANES, 2 * LANES), 0) + y * LANES
    lane2 = iota((2 * LANES, 2 * LANES), 1)
    inner = lane2 % LANES
    head = jnp.where(lane2 < LANES, s, mate)
    pick = jnp.where((inner < HD) & (feature == head * HD + inner), 1.0, 0.0).astype(BF)
    for i in range(3):

        def pick_rows(r, carry, i=i):
            rows = pl.ds(pl.multiple_of(r * 256, 256), 256)
            part = dot(qkvw[i, rows, :], pick).astype(BF)
            wsel[rows, i * LANES : (i + 1) * LANES] = part[:, :LANES]
            wsel[rows, (3 + i) * LANES : (4 + i) * LANES] = part[:, LANES:]
            return carry

        lax.fori_loop(0, D // 256, pick_rows, 0)

    for ld in loads[5:12]:
        ld.wait()
    for k in range(1, SEQ):
        x_copy(k, (s - k + SEQ) % SEQ).wait_recv()

    def w2_copy(k, source):
        return rcopy(
            wx.at[xx] if source is None else wx.at[xx],
            wx.at[xx if source is None else source],
            w2_s.at[k],
            w2_r.at[k],
            dpi(z, (xx + k) % XN),
            s,
        )

    def wt_rows(zz):
        return wt.at[pl.ds(pl.multiple_of(zz * 160, 32), 160), :]

    def w3_copy(k, source):
        block = wt_rows(source)
        return rcopy(block, block, w3_s.at[k], w3_r.at[k], dp, ((y + k) % YN) * 2 + c)

    def w4_copy(k, core):
        block = wt_rows(((y - k + YN) % YN) * 2 + core)
        return rcopy(block, block, w4_s.at[k], w4_r.at[k], dp, mate)

    def m_copy(i, core):
        rows = pl.multiple_of((2 * i + core) * ROWS, ROWS)
        return rcopy(msend.at[i], qkv.at[pl.ds(rows, ROWS), :], m_s.at[i], m_r.at[i], dp, mate)

    lane = iota((ROWS, LANES), 1)
    seg_lane = (lane >= HD) & (lane < HD + 16)

    def embed_chunk(i):
        chunk = 2 * i + c
        first_row = pl.multiple_of(chunk * ROWS, ROWS)
        pos = first_row + iota((ROWS, 64), 0)
        source, first, count = plan_ref[0], plan_ref[1], plan_ref[2]
        start = plan_ref[3] * ROWS + plan_ref[4]
        inside = (pos >= start) & (pos < start + count)
        code = jnp.where(inside, (source * 512 + first - start) + pos, 0)
        code = jnp.sum(code.astype(F32), axis=1, keepdims=True).astype(jnp.int32)
        row_of = code % 512
        shard_of = code // 512
        onehot = jnp.where(iota((ROWS, ROWS), 1) == row_of, 1.0, 0.0).astype(BF)
        spread = dot_nt(onehot, xg[...])
        cols = jnp.where(
            iota((ROWS, SEQ * PATCH), 1) // PATCH == shard_of, spread, 0.0
        ).astype(BF)
        half = (dot(cols, win8[...]) + bin_ref[...].reshape(1, D)) * 0.5
        hidden = (half + half * jnp.tanh(half)).astype(BF)
        emb = (dot(hidden, wh[...]) + dot(cols, wskip8[...]) + ob_ref[...].reshape(1, D)).astype(BF)

        emb_own[i] = emb

        wide = emb.astype(F32)
        scale = lax.rsqrt(jnp.mean(wide * wide, axis=-1, keepdims=True) + EPS)
        normed = (wide * scale * gain_ref[...].reshape(1, D)).astype(BF)
        proj = dot(normed, wsel[...]).astype(BF)

        seg_row = seg_ref[:, pl.ds(first_row, ROWS)]
        marks = jnp.where(iota((LANES, ROWS), 0) - HD == seg_row, 1.0, 0.0)
        marks = jnp.transpose(marks)
        away = jnp.where(seg_lane, (marks - 1.0) * MASKED, 0.0)
        ones = jnp.where(lane == HD, 1.0, 0.0)
        parts = []
        for h in range(2):
            q = proj[:, (3 * h) * LANES : (3 * h + 1) * LANES].astype(F32)
            k = proj[:, (3 * h + 1) * LANES : (3 * h + 2) * LANES].astype(F32)
            v = proj[:, (3 * h + 2) * LANES : (3 * h + 3) * LANES].astype(F32)
            q = q * lax.rsqrt(jnp.sum(q * q, axis=-1, keepdims=True) * (1.0 / HD) + EPS)
            k = k * lax.rsqrt(jnp.sum(k * k, axis=-1, keepdims=True) * (1.0 / HD) + EPS)
            parts.append([(q + away).astype(BF), (k + marks).astype(BF), (v + ones).astype(BF)])
        for j in range(3):
            msend[i, :, j * LANES : (j + 1) * LANES] = parts[1][j]
        m_copy(i, c).start()
        for j in range(3):
            qkv[pl.ds(first_row, ROWS), j * LANES : (j + 1) * LANES] = parts[0][j]

    embed_chunk(0)
    for k in range(1, ZN):
        w1_copy(k, (z - k + ZN) % ZN).wait_recv()
    for m in range(5):
        tiles[m] = w_land[:, m * LANES : (m + 1) * LANES]
    block = jnp.concatenate(
        [
            jnp.concatenate([tiles[m, pl.ds(j, ZN, stride=8), :] for j in range(COLS)], axis=0)
            for m in range(5)
        ],
        axis=1,
    )
    block = jnp.concatenate([block, jnp.zeros((8, HW), F32)], axis=0)
    wx[xx] = block.astype(BF)
    for k in range(1, XN):
        w2_copy(k, None).start()
    embed_chunk(1)
    for k in range(1, XN):
        w2_copy(k, (xx - k + XN) % XN).wait_recv()
    block = jnp.concatenate([wx[j, 0:GROUP, :].astype(F32) for j in range(XN)], axis=0)
    wt[pl.ds(pl.multiple_of(s * 160, 32), 160), :] = block.astype(BF)
    for k in range(1, YN):
        w3_copy(k, s).start()
    w4_copy(0, c).start()
    embed_chunk(2)
    embed_chunk(3)
    for i in range(4):
        m_copy(i, 1 - c).wait_recv()

    factor = hs_ref[s] * (LOG2E / math.sqrt(HD))
    causal = iota((ROWS, ROWS), 0) >= iota((ROWS, ROWS), 1)

    def a_copy(block, source, k):
        rows = ret.at[pl.ds(pl.multiple_of(source * HD, 16), HD), :]
        return rcopy(att_send.at[block], rows, a_s.at[k], a_r.at[k], dp, (s + k) % SEQ)

    for b in reversed(range(SEQ)):
        q = qkv[b * ROWS : (b + 1) * ROWS, 0:LANES]
        total = jnp.zeros((ROWS, LANES), F32)
        edges = list(range(0, b * ROWS, 2 * ROWS)) + [b * ROWS]
        for lo, hi in zip(edges[:-1], edges[1:]):
            scores = dot_nt(q, qkv[lo:hi, LANES : 2 * LANES]) * factor
            total = total + dot(jnp.exp2(scores).astype(BF), qkv[lo:hi, 2 * LANES : 3 * LANES])
        lo, hi = b * ROWS, (b + 1) * ROWS
        scores = dot_nt(q, qkv[lo:hi, LANES : 2 * LANES]) * factor
        weights = jnp.where(causal, jnp.exp2(scores), 0.0).astype(BF)
        total = total + dot(weights, qkv[lo:hi, 2 * LANES : 3 * LANES])
        across = jnp.transpose(total)
        out = (across[0:HD, :] / across[HD : HD + 1, :]).astype(BF)
        att_send[b] = out

        @pl.when(s == b)
        def _():
            ret[pl.ds(pl.multiple_of(s * HD, 16), HD), :] = out

        @pl.when(s != b)
        def _():
            a_copy(b, s, (b - s + SEQ) % SEQ).start()

        if b == 3:
            for k in range(1, YN):
                w3_copy(k, ((y - k + YN) % YN) * 2 + c).wait_recv()
                w4_copy(k, c).start()

    loads[12].wait()
    for m in range(3):
        cot_f[m] = jnp.transpose(cot[m * LANES : (m + 1) * LANES, :].astype(F32))
    for core in range(2):
        for j in range(YN):
            base = [x2 * GROUP + (2 * j + core) * COLS + n for x2 in range(XN) for n in range(COLS)]
            for m in range(3):
                rows = [cot_f[m, pl.ds(first, ZN, stride=160), :] for first in base]
                rows = jnp.concatenate(rows, axis=0).astype(BF)
                cot_t[core, j * 160 : (j + 1) * 160, m * LANES : (m + 1) * LANES] = rows
    for k in range(YN):
        w4_copy(k, 1 - c).wait_recv()
    for t in range(SEQ):
        block = wt[t * 160 : (t + 1) * 160, :].astype(F32)
        for x2 in range(XN):
            for n in range(COLS):
                first = x2 * GROUP + n * ZN
                rows = pl.ds(x2 * GROUP + t * COLS + n, ZN, stride=160)
                for m in range(5):
                    wt_f[m, rows, :] = block[first : first + ZN, m * LANES : (m + 1) * LANES]

    for k in range(1, SEQ):
        a_copy(0, (s - k + SEQ) % SEQ, k).wait_recv()

    attended = ret[...]
    order = [2, 1, 3, 0]

    def p_copy(k):
        piece = (y + k) % YN
        return rcopy(p_send.at[piece], p_land.at[piece], p_s.at[k], p_r.at[k], dp, mate)

    def owner_rows(k):
        return pl.ds(pl.multiple_of(((y + k) % YN) * 160, 32), 160)

    for k in order:
        p_send[(y + k) % YN] = dot_nt(cot_t[1 - c, owner_rows(k), :], attended).astype(BF)
        p_copy(k).start()
    p_own[...] = dot_nt(cot_t[c], attended)

    def ya_copy(k):
        to = (y + k) % YN
        return rcopy(ya.at[to], ya_land.at[k], ya_s.at[k], ya_r.at[k], dp, to * 2 + c)

    def xb_copy(k):
        to = (xx + k) % XN
        return rcopy(xb.at[to], xb_land.at[k], xb_s.at[k], xb_r.at[k], dpi(z, to), s)

    pad = jnp.zeros((8, HW - ROWS), F32)
    for k in order:
        to = (y + k) % YN
        p_copy(k).wait_recv()
        piece = p_own[owner_rows(k), :] + p_land[to].astype(F32)
        p_own[owner_rows(k), :] = piece
        if k:
            ya[to] = piece[:, 0:ROWS].astype(BF)
            ya_copy(k).start()
        for j in range(XN):
            part = piece[j * GROUP : (j + 1) * GROUP, ROWS:]
            xb[j, to] = jnp.concatenate([part, pad], axis=0).astype(BF)
    for k in (2, 1, 3):
        xb_copy(k).start()

    rows = jnp.transpose(attended)
    for j in range(5):
        cols = slice(j * 256, (j + 1) * 256)
        weight = jnp.concatenate([wt_f[m, cols, :].astype(BF) for m in range(5)], axis=1)
        branch = dot_nt(rows, weight)
        lo_ref[:, cols] = (emb_own[y, :, cols].astype(F32) + branch).astype(BF)

    for k in range(1, YN):
        ya_copy(k).wait_recv()
    own = p_own[pl.ds(pl.multiple_of(y * 160, 32), 160), :]
    a_sum = own[:, 0:ROWS]
    for k in range(1, YN):
        a_sum = a_sum + ya_land[k].astype(F32)
    pad = jnp.zeros((8, ROWS), F32)
    block40[...] = jnp.zeros_like(block40)
    for j in range(XN):
        piece = a_sum[j * GROUP : (j + 1) * GROUP, :]
        ax[j] = jnp.concatenate([piece, pad], axis=0).astype(BF)

        @pl.when(xx == j)
        def _():
            block40[:, 0:ROWS] = piece

    def ax_copy(k):
        to = (xx + k) % XN
        return rcopy(ax.at[to], ax_land.at[k], ax_s.at[k], ax_r.at[k], dpi(z, to), s)

    for k in range(1, XN):
        ax_copy(k).start()

    for k in range(1, XN):
        xb_copy(k).wait_recv()
    pad = jnp.zeros((8, HW - ROWS), F32)
    for j in range(YN):
        begin = pl.multiple_of((j * XN + xx) * GROUP, 8)
        piece = p_own[pl.ds(begin, GROUP), ROWS:HW]
        for k in range(1, XN):
            piece = piece + xb_land[k, j].astype(F32)[0:GROUP, :]
        by[j] = jnp.concatenate([piece, pad], axis=0).astype(BF)

        @pl.when(y == j)
        def _():
            block40[:, ROWS:HW] = piece

    def by_copy(k):
        to = (y + k) % YN
        return rcopy(by.at[to], by_land.at[k], by_s.at[k], by_r.at[k], dp, to * 2 + c)

    for k in range(1, YN):
        by_copy(k).start()
    for k in range(1, XN):
        ax_copy(k).wait_recv()
    for k in range(1, YN):
        by_copy(k).wait_recv()
    left = block40[:, 0:ROWS]
    right = block40[:, ROWS:HW]
    for k in range(1, XN):
        left = left + ax_land[k].astype(F32)[0:GROUP, :]
        right = right + by_land[k].astype(F32)[0:GROUP, :]
    block40[:, 0:ROWS] = left
    block40[:, ROWS:HW] = right
    for m in range(5):
        tiles[m, 0:GROUP, :] = block40[:, m * LANES : (m + 1) * LANES]
    for j in range(ZN):
        for m in range(5):
            part = tiles[m, pl.ds(j, COLS, stride=ZN), :]
            fs_f[j, m * COLS : (m + 1) * COLS, :] = part
    fs[...] = fs_f[...].astype(BF)

    def f_copy(k):
        to = (z + k) % ZN
        return rcopy(fs.at[to], fs_land.at[k], f_s.at[k], f_r.at[k], dpi(to, xx), s)

    for k in (4, 3, 5, 2, 6, 1, 7):
        f_copy(k).start()
    final = fs_f[z]
    for k in range(1, ZN):
        f_copy(k).wait_recv()
        final = final + fs_land[k].astype(F32)
    fs_f[0] = final
    for m in range(COLS):
        og_ref[:, m * LANES : (m + 1) * LANES] = fs_f[0, m * COLS : (m + 1) * COLS, :]

    for k in range(1, SEQ):
        x_copy(k, s).wait_send()
        a_copy(0, s, k).wait_send()
    for k in range(1, ZN):
        w1_copy(k, z).wait_send()
        f_copy(k).wait_send()
    for k in range(1, XN):
        w2_copy(k, None).wait_send()
        w3_copy(k, s).wait_send()
        ya_copy(k).wait_send()
        xb_copy(k).wait_send()
        ax_copy(k).wait_send()
        by_copy(k).wait_send()
    for k in range(YN):
        w4_copy(k, c).wait_send()
        m_copy(k, c).wait_send()
        p_copy(k).wait_send()


def per_device(
    patches,
    segment_ids,
    regroup_plan,
    input_weight,
    input_bias,
    skip_weight,
    hidden_weight,
    output_bias,
    norm_gain,
    head_scale,
    qkv_weight,
    out_weight,
    cotangent,
):
    vmem = pl.BlockSpec(memory_space=pltpu.VMEM)
    hbm = pl.BlockSpec(memory_space=pltpu.HBM)
    dma = pltpu.SemaphoreType.DMA
    scratch = [
        pltpu.VMEM((PATCH, ROWS), BF),
        pltpu.VMEM((1, WIN), jnp.int32),
        pltpu.VMEM((5, 1, 64), jnp.int32),
        pltpu.VMEM((PATCH, D), BF),
        pltpu.VMEM((D,), F32),
        pltpu.VMEM((PATCH, D), BF),
        pltpu.VMEM((D,), F32),
        pltpu.VMEM((D,), F32),
        pltpu.SMEM((SEQ,), F32),
        pltpu.VMEM((COLS, HW), BF),
        pltpu.VMEM((D, D), BF),
        pltpu.VMEM((3, D, 2 * LANES), BF),
        pltpu.VMEM((ROWS, D), BF),
        pltpu.VMEM((3, D, LANES), F32),
        pltpu.VMEM((2, HW, ROWS), BF),
        pltpu.VMEM((SEQ * PATCH, ROWS), BF),
        pltpu.VMEM((SEQ * PATCH, D), BF),
        pltpu.VMEM((SEQ * PATCH, D), BF),
        pltpu.VMEM((D, 6 * LANES), BF),
        pltpu.VMEM((WIN, 3 * LANES), BF),
        pltpu.VMEM((4, ROWS, 3 * LANES), BF),
        pltpu.VMEM((4, ROWS, D), BF),
        pltpu.VMEM((8, HW), F32),
        pltpu.VMEM((ZN * 8, HW), F32),
        pltpu.VMEM((XN, 48, HW), BF),
        pltpu.VMEM((D, HW), BF),
        pltpu.VMEM((5, D, LANES), F32),
        pltpu.VMEM((5, 64, LANES), F32),
        pltpu.VMEM((SEQ, HD, ROWS), BF),
        pltpu.VMEM((HW, ROWS), BF),
        pltpu.VMEM((HW, HW), F32),
        pltpu.VMEM((YN, 160, HW), BF),
        pltpu.VMEM((YN, 160, HW), BF),
        pltpu.VMEM((YN, 160, ROWS), BF),
        pltpu.VMEM((YN, 160, ROWS), BF),
        pltpu.VMEM((XN, YN, 48, HW - ROWS), BF),
        pltpu.VMEM((XN, YN, 48, HW - ROWS), BF),
        pltpu.VMEM((XN, 48, ROWS), BF),
        pltpu.VMEM((XN, 48, ROWS), BF),
        pltpu.VMEM((YN, 48, HW - ROWS), BF),
        pltpu.VMEM((YN, 48, HW - ROWS), BF),
        pltpu.VMEM((GROUP, HW), F32),
        pltpu.VMEM((ZN, 32, LANES), F32),
        pltpu.VMEM((ZN, 32, LANES), BF),
        pltpu.VMEM((ZN, 32, LANES), BF),
        dma((13,)),
        dma((8,)),
        dma((8,)),
        dma((8,)),
        dma((8,)),
        dma((4,)),
        dma((4,)),
        dma((4,)),
        dma((4,)),
        dma((4,)),
        dma((4,)),
        dma((4,)),
        dma((4,)),
        dma((8,)),
        dma((8,)),
        dma((4,)),
        dma((4,)),
        dma((4,)),
        dma((4,)),
        dma((4,)),
        dma((4,)),
        dma((4,)),
        dma((4,)),
        dma((4,)),
        dma((4,)),
        dma((8,)),
        dma((8,)),
    ]
    layer_out, grad = pl.pallas_call(
        whole_layer,
        out_shape=(
            jax.ShapeDtypeStruct((ROWS, D), BF),
            jax.ShapeDtypeStruct((COLS, HW), F32),
        ),
        in_specs=[hbm] * 13,
        out_specs=(vmem, vmem),
        scratch_shapes=scratch,
        compiler_params=pltpu.CompilerParams(
            collective_id=0, has_side_effects=True, vmem_limit_bytes=63 * 1024 * 1024
        ),
        name="whole_layer",
    )(
        patches,
        segment_ids,
        jnp.transpose(regroup_plan, (1, 0, 2)),
        input_weight,
        input_bias,
        skip_weight,
        hidden_weight,
        output_bias,
        norm_gain,
        head_scale,
        jnp.transpose(qkv_weight, (1, 0, 2)),
        jnp.transpose(out_weight),
        cotangent,
    )
    return layer_out, jnp.transpose(grad)


def solution(mesh):
    placed = (
        P(None, ("dp", "seq")),
        P("dp", None),
        P("dp", None, None),
        P(),
        P(),
        P(),
        P(),
        P(),
        P(),
        P(),
        P(),
        P(None, ("dp", "seq")),
        P(("dp", "seq"), None),
    )
    return jax.shard_map(
        per_device,
        mesh=mesh,
        in_specs=placed,
        out_specs=(P(("dp", "seq"), None), P(None, ("dp", "seq"))),
        check_vma=False,
    )
```

```python
import functools
import math

import jax
import jax.numpy as jnp
from jax import lax
from jax.experimental import pallas as pl
from jax.experimental.pallas import tpu as pltpu
from jax.sharding import PartitionSpec as P

HD = 80
LANES = 128
ZN, XN, YN = 8, 4, 4
SEQ = 8
ROWS = 384
WIN = ROWS * SEQ
D = 1280
HW = 640
PATCH = 32
COLS = 5
GROUP = COLS * SEQ
EPS = 1e-06
MASKED = 2048.0
LOG2E = 1.4426950408889634
MESH = pl.DeviceIdType.MESH
BF = jnp.bfloat16
F32 = jnp.float32
NT = (((1,), (1,)), ((), ()))


def iota(shape, dim):
    return lax.broadcasted_iota(jnp.int32, shape, dim)


def dot(a, b):
    return jnp.dot(a, b, preferred_element_type=F32)


def dot_nt(a, b):
    return lax.dot_general(a, b, NT, preferred_element_type=F32)


def whole_layer(
    x_hbm,
    seg_hbm,
    plan_hbm,
    win_hbm,
    bin_hbm,
    wskip_hbm,
    wh_hbm,
    ob_hbm,
    gain_hbm,
    hs_hbm,
    qkvw_hbm,
    ow_hbm,
    cot_hbm,
    lo_ref,
    og_ref,
    seg_ref,
    plan_ref,
    win_ref,
    bin_ref,
    wskip_ref,
    ob_ref,
    gain_ref,
    hs_ref,
    ow_ref,
    wh,
    qkvw,
    cot,
    cot_f,
    cot_t,
    xg,
    win8,
    wskip8,
    wsel,
    qkv,
    msend,
    emb_own,
    ow_send,
    w_land,
    wx,
    wt,
    wt_f,
    tiles,
    att_send,
    ret,
    p_own,
    p_send,
    p_land,
    ya,
    ya_land,
    xb,
    xb_land,
    ax,
    ax_land,
    by,
    by_land,
    block40,
    fs_f,
    fs,
    fs_land,
    ld_sem,
    x_s,
    x_r,
    w1_s,
    w1_r,
    w2_s,
    w2_r,
    w3_s,
    w3_r,
    w4_s,
    w4_r,
    m_s,
    m_r,
    a_s,
    a_r,
    p_s,
    p_r,
    ya_s,
    ya_r,
    xb_s,
    xb_r,
    ax_s,
    ax_r,
    by_s,
    by_r,
    f_s,
    f_r,
):
    dp = lax.axis_index("dp")
    s = lax.axis_index("seq")
    z = dp // XN
    xx = dp % XN
    y = s // 2
    c = s % 2
    mate = y * 2 + (1 - c)
    def rcopy(src, dst, ssem, rsem, dp_t, seq_t):
        return pltpu.make_async_remote_copy(
            src_ref=src,
            dst_ref=dst,
            send_sem=ssem,
            recv_sem=rsem,
            device_id=(dp_t, seq_t),
            device_id_type=MESH,
        )

    def dpi(zz, x2):
        return zz * XN + x2

    bar = pltpu.get_barrier_semaphore()

    def greet(dp_t, seq_t):
        pl.semaphore_signal(bar, inc=1, device_id=(dp_t, seq_t), device_id_type=MESH)

    for k in range(1, SEQ):
        greet(dp, (s + k) % SEQ)
    for k in range(1, XN):
        greet(dpi(z, (xx + k) % XN), s)
    for k in range(1, ZN):
        greet(dpi((z + k) % ZN, xx), s)

    loads = [
        pltpu.make_async_copy(src, dst, ld_sem.at[i])
        for i, (src, dst) in enumerate(
            [
                (x_hbm, xg.at[pl.ds(pl.multiple_of(s * PATCH, PATCH), PATCH), :]),
                (ow_hbm, ow_ref),
                (win_hbm, win_ref),
                (wskip_hbm, wskip_ref),
                (qkvw_hbm.at[:, :, pl.ds(pl.multiple_of(y * LANES, LANES), 2 * LANES)], qkvw),
                (plan_hbm, plan_ref),
                (seg_hbm, seg_ref),
                (bin_hbm, bin_ref),
                (ob_hbm, ob_ref),
                (gain_hbm, gain_ref),
                (hs_hbm, hs_ref),
                (wh_hbm, wh),
                (cot_hbm, cot),
            ]
        )
    ]
    for ld in loads:
        ld.start()

    pl.semaphore_wait(bar, 7 + 3 + 7)

    def x_copy(k, source):
        rows = xg.at[pl.ds(pl.multiple_of(source * PATCH, PATCH), PATCH), :]
        return rcopy(x_hbm, rows, x_s.at[k], x_r.at[k], dp, (s + k) % SEQ)

    for k in range(1, SEQ):
        x_copy(k, s).start()

    for ld in loads[1:2]:
        ld.wait()
    ow_send[...] = jnp.zeros((8, HW), F32)
    ow_send[0:COLS, :] = ow_ref[...].astype(F32)

    def w1_copy(k, source):
        slot = w_land.at[pl.ds(pl.multiple_of(source * 8, 8), 8), :]
        return rcopy(ow_send, slot, w1_s.at[k], w1_r.at[k], dpi((z + k) % ZN, xx), s)

    for k in range(1, ZN):
        w1_copy(k, z).start()
    w_land[pl.ds(pl.multiple_of(z * 8, 8), 8), :] = ow_send[...]

    for ld in (loads[0], *loads[2:4]):
        ld.wait()
    for k in range(SEQ):
        win8[k * PATCH : (k + 1) * PATCH, :] = win_ref[...]
        wskip8[k * PATCH : (k + 1) * PATCH, :] = wskip_ref[...]

    loads[4].wait()
    feature = iota((2 * LANES, 2 * LANES), 0) + y * LANES
    lane2 = iota((2 * LANES, 2 * LANES), 1)
    inner = lane2 % LANES
    head = jnp.where(lane2 < LANES, s, mate)
    pick = jnp.where((inner < HD) & (feature == head * HD + inner), 1.0, 0.0).astype(BF)
    for i in range(3):
        part = dot(qkvw[i], pick).astype(BF)
        wsel[:, i * LANES : (i + 1) * LANES] = part[:, :LANES]
        wsel[:, (3 + i) * LANES : (4 + i) * LANES] = part[:, LANES:]
    for ld in loads[5:12]:
        ld.wait()
    for k in range(1, SEQ):
        x_copy(k, (s - k + SEQ) % SEQ).wait_recv()

    def w2_copy(k, source):
        return rcopy(
            wx.at[xx] if source is None else wx.at[xx],
            wx.at[xx if source is None else source],
            w2_s.at[k],
            w2_r.at[k],
            dpi(z, (xx + k) % XN),
            s,
        )

    def wt_rows(zz):
        return wt.at[pl.ds(pl.multiple_of(zz * 160, 32), 160), :]

    def w3_copy(k, source):
        block = wt_rows(source)
        return rcopy(block, block, w3_s.at[k], w3_r.at[k], dp, ((y + k) % YN) * 2 + c)

    def w4_copy(k, core):
        block = wt_rows(((y - k + YN) % YN) * 2 + core)
        return rcopy(block, block, w4_s.at[k], w4_r.at[k], dp, mate)

    def m_copy(i, core):
        rows = pl.multiple_of((2 * i + core) * ROWS, ROWS)
        return rcopy(msend.at[i], qkv.at[pl.ds(rows, ROWS), :], m_s.at[i], m_r.at[i], dp, mate)

    lane = iota((2 * ROWS, LANES), 1)
    seg_lane = (lane >= HD) & (lane < HD + 16)

    def embed_rows(g):
        begin = [pl.multiple_of((4 * g + 2 * e + c) * ROWS, ROWS) for e in range(2)]
        step = iota((2 * ROWS, 64), 0)
        pos = begin[0] + step + jnp.where(step >= ROWS, ROWS, 0)
        source, first, count = plan_ref[0], plan_ref[1], plan_ref[2]
        start = plan_ref[3] * ROWS + plan_ref[4]
        inside = (pos >= start) & (pos < start + count)
        code = jnp.where(inside, (source * 512 + first - start) + pos, 0)
        code = jnp.sum(code.astype(F32), axis=1, keepdims=True).astype(jnp.int32)
        row_of = code % 512
        shard_of = code // 512
        onehot = jnp.where(iota((2 * ROWS, ROWS), 1) == row_of, 1.0, 0.0).astype(BF)
        spread = dot_nt(onehot, xg[...])
        cols = jnp.where(
            iota((2 * ROWS, SEQ * PATCH), 1) // PATCH == shard_of, spread, 0.0
        ).astype(BF)
        half = (dot(cols, win8[...]) + bin_ref[...].reshape(1, D)) * 0.5
        hidden = (half + half * jnp.tanh(half)).astype(BF)
        emb = dot(hidden, wh[...]) + dot(cols, wskip8[...]) + ob_ref[...].reshape(1, D)
        emb = emb.astype(BF)
        emb_own[2 * g] = emb[:ROWS]
        emb_own[2 * g + 1] = emb[ROWS:]
        return begin, emb

    def project_rows(g, begin, emb):
        wide = emb.astype(F32)
        scale = lax.rsqrt(jnp.mean(wide * wide, axis=-1, keepdims=True) + EPS)
        normed = (wide * scale * gain_ref[...].reshape(1, D)).astype(BF)
        proj = dot(normed, wsel[...]).astype(BF)

        marks = []
        for e in range(2):
            seg_row = seg_ref[:, pl.ds(begin[e], ROWS)]
            match = jnp.where(iota((LANES, ROWS), 0) - HD == seg_row, 1.0, 0.0)
            marks.append(jnp.transpose(match))
        marks = jnp.concatenate(marks, axis=0)
        away = jnp.where(seg_lane, (marks - 1.0) * MASKED, 0.0)
        ones = jnp.where(lane == HD, 1.0, 0.0)
        for h in (1, 0):
            q = proj[:, (3 * h) * LANES : (3 * h + 1) * LANES].astype(F32)
            k = proj[:, (3 * h + 1) * LANES : (3 * h + 2) * LANES].astype(F32)
            v = proj[:, (3 * h + 2) * LANES : (3 * h + 3) * LANES].astype(F32)
            q = q * lax.rsqrt(jnp.sum(q * q, axis=-1, keepdims=True) * (1.0 / HD) + EPS)
            k = k * lax.rsqrt(jnp.sum(k * k, axis=-1, keepdims=True) * (1.0 / HD) + EPS)
            parts = [(q + away).astype(BF), (k + marks).astype(BF), (v + ones).astype(BF)]
            for e in range(2):
                for j in range(3):
                    part = parts[j][e * ROWS : (e + 1) * ROWS]
                    lanes = slice(j * LANES, (j + 1) * LANES)
                    if h:
                        msend[2 * g + e, :, lanes] = part
                    else:
                        qkv[pl.ds(begin[e], ROWS), lanes] = part
            if h:
                m_copy(2 * g, c).start()
                m_copy(2 * g + 1, c).start()

    begin, emb = embed_rows(0)
    for k in range(1, ZN):
        w1_copy(k, (z - k + ZN) % ZN).wait_recv()
    for m in range(5):
        tiles[m] = w_land[:, m * LANES : (m + 1) * LANES]
    block = jnp.concatenate(
        [
            jnp.concatenate([tiles[m, pl.ds(j, ZN, stride=8), :] for j in range(COLS)], axis=0)
            for m in range(5)
        ],
        axis=1,
    )
    block = jnp.concatenate([block, jnp.zeros((8, HW), F32)], axis=0)
    wx[xx] = block.astype(BF)
    for k in range(1, XN):
        w2_copy(k, None).start()
    project_rows(0, begin, emb)
    for k in range(1, XN):
        w2_copy(k, (xx - k + XN) % XN).wait_recv()
    block = jnp.concatenate([wx[j, 0:GROUP, :].astype(F32) for j in range(XN)], axis=0)
    wt[pl.ds(pl.multiple_of(s * 160, 32), 160), :] = block.astype(BF)
    for k in range(1, YN):
        w3_copy(k, s).start()
    w4_copy(0, c).start()
    project_rows(1, *embed_rows(1))
    factor = hs_ref[s] * (LOG2E / math.sqrt(HD))
    causal = iota((ROWS, ROWS), 0) >= iota((ROWS, ROWS), 1)

    def a_copy(block, source, k):
        rows = ret.at[pl.ds(pl.multiple_of(source * HD, 16), HD), :]
        return rcopy(att_send.at[block], rows, a_s.at[k], a_r.at[k], dp, (s + k) % SEQ)

    for i in range(2):
        m_copy(i, 1 - c).wait_recv()
    for b in (3, 2, 7, 0, 5, 1, 6, 4):
        if b == 7:
            for i in range(2, 4):
                m_copy(i, 1 - c).wait_recv()
        q = qkv[b * ROWS : (b + 1) * ROWS, 0:LANES]
        total = jnp.zeros((ROWS, LANES), F32)
        edges = list(range(0, b * ROWS, 2 * ROWS)) + [b * ROWS]
        for lo, hi in zip(edges[:-1], edges[1:]):
            scores = dot_nt(q, qkv[lo:hi, LANES : 2 * LANES]) * factor
            total = total + dot(jnp.exp2(scores).astype(BF), qkv[lo:hi, 2 * LANES : 3 * LANES])
        lo, hi = b * ROWS, (b + 1) * ROWS
        scores = dot_nt(q, qkv[lo:hi, LANES : 2 * LANES]) * factor
        weights = jnp.where(causal, jnp.exp2(scores), 0.0).astype(BF)
        total = total + dot(weights, qkv[lo:hi, 2 * LANES : 3 * LANES])
        across = jnp.transpose(total)
        out = (across[0:HD, :] / across[HD : HD + 1, :]).astype(BF)
        att_send[b] = out

        @pl.when(s == b)
        def _():
            ret[pl.ds(pl.multiple_of(s * HD, 16), HD), :] = out

        @pl.when(s != b)
        def _():
            a_copy(b, s, (b - s + SEQ) % SEQ).start()

        if b == 5:
            for k in range(1, YN):
                w3_copy(k, ((y - k + YN) % YN) * 2 + c).wait_recv()
                w4_copy(k, c).start()

    loads[12].wait()
    for m in range(3):
        cot_f[m] = jnp.transpose(cot[m * LANES : (m + 1) * LANES, :].astype(F32))
    for core in range(2):
        for j in range(YN):
            base = [x2 * GROUP + (2 * j + core) * COLS + n for x2 in range(XN) for n in range(COLS)]
            for m in range(3):
                rows = [cot_f[m, pl.ds(first, ZN, stride=160), :] for first in base]
                rows = jnp.concatenate(rows, axis=0).astype(BF)
                cot_t[core, j * 160 : (j + 1) * 160, m * LANES : (m + 1) * LANES] = rows
    for k in range(YN):
        w4_copy(k, 1 - c).wait_recv()
    for t in range(SEQ):
        block = wt[t * 160 : (t + 1) * 160, :].astype(F32)
        for x2 in range(XN):
            for n in range(COLS):
                first = x2 * GROUP + n * ZN
                rows = pl.ds(x2 * GROUP + t * COLS + n, ZN, stride=160)
                for m in range(5):
                    wt_f[m, rows, :] = block[first : first + ZN, m * LANES : (m + 1) * LANES]

    for k in range(1, SEQ):
        a_copy(0, (s - k + SEQ) % SEQ, k).wait_recv()

    attended = ret[...]
    order = [2, 1, 3, 0]

    def p_copy(k):
        piece = (y + k) % YN
        return rcopy(p_send.at[piece], p_land.at[piece], p_s.at[k], p_r.at[k], dp, mate)

    def owner_rows(k):
        return pl.ds(pl.multiple_of(((y + k) % YN) * 160, 32), 160)

    for k in order:
        p_send[(y + k) % YN] = dot_nt(cot_t[1 - c, owner_rows(k), :], attended).astype(BF)
        p_copy(k).start()
    p_own[...] = dot_nt(cot_t[c], attended)

    def ya_copy(k):
        to = (y + k) % YN
        return rcopy(ya.at[to], ya_land.at[k], ya_s.at[k], ya_r.at[k], dp, to * 2 + c)

    def xb_copy(k, row):
        to = (xx + k) % XN
        slot = k * YN + row
        return rcopy(
            xb.at[to, row], xb_land.at[k, row], xb_s.at[slot], xb_r.at[slot], dpi(z, to), s
        )

    pad = jnp.zeros((8, HW - ROWS), F32)
    for k in order:
        to = (y + k) % YN
        p_copy(k).wait_recv()
        piece = p_own[owner_rows(k), :] + p_land[to].astype(F32)
        p_own[owner_rows(k), :] = piece
        if k:
            ya[to] = piece[:, 0:ROWS].astype(BF)
            ya_copy(k).start()
        for j in range(XN):
            part = piece[j * GROUP : (j + 1) * GROUP, ROWS:]
            xb[j, to] = jnp.concatenate([part, pad], axis=0).astype(BF)
        for j in (2, 1, 3):
            xb_copy(j, to).start()

    rows = jnp.transpose(attended)
    for j in range(5):
        cols = slice(j * 256, (j + 1) * 256)
        weight = jnp.concatenate([wt_f[m, cols, :].astype(BF) for m in range(5)], axis=1)
        branch = dot_nt(rows, weight)
        lo_ref[:, cols] = (emb_own[y, :, cols].astype(F32) + branch).astype(BF)

    for k in range(1, YN):
        ya_copy(k).wait_recv()
    own = p_own[pl.ds(pl.multiple_of(y * 160, 32), 160), :]
    a_sum = own[:, 0:ROWS]
    for k in range(1, YN):
        a_sum = a_sum + ya_land[k].astype(F32)
    pad = jnp.zeros((8, ROWS), F32)
    block40[...] = jnp.zeros_like(block40)
    for j in range(XN):
        piece = a_sum[j * GROUP : (j + 1) * GROUP, :]
        ax[j] = jnp.concatenate([piece, pad], axis=0).astype(BF)

        @pl.when(xx == j)
        def _():
            block40[:, 0:ROWS] = piece

    def ax_copy(k):
        to = (xx + k) % XN
        return rcopy(ax.at[to], ax_land.at[k], ax_s.at[k], ax_r.at[k], dpi(z, to), s)

    for k in range(1, XN):
        ax_copy(k).start()

    for k in range(1, XN):
        for j in range(YN):
            xb_copy(k, j).wait_recv()
    pad = jnp.zeros((8, HW - ROWS), F32)
    for j in range(YN):
        begin = pl.multiple_of((j * XN + xx) * GROUP, 8)
        piece = p_own[pl.ds(begin, GROUP), ROWS:HW]
        for k in range(1, XN):
            piece = piece + xb_land[k, j].astype(F32)[0:GROUP, :]
        by[j] = jnp.concatenate([piece, pad], axis=0).astype(BF)

        @pl.when(y == j)
        def _():
            block40[:, ROWS:HW] = piece

    def by_copy(k):
        to = (y + k) % YN
        return rcopy(by.at[to], by_land.at[k], by_s.at[k], by_r.at[k], dp, to * 2 + c)

    for k in range(1, YN):
        by_copy(k).start()
    for k in range(1, XN):
        ax_copy(k).wait_recv()
    for k in range(1, YN):
        by_copy(k).wait_recv()
    left = block40[:, 0:ROWS]
    right = block40[:, ROWS:HW]
    for k in range(1, XN):
        left = left + ax_land[k].astype(F32)[0:GROUP, :]
        right = right + by_land[k].astype(F32)[0:GROUP, :]
    block40[:, 0:ROWS] = left
    block40[:, ROWS:HW] = right
    for m in range(5):
        tiles[m, 0:GROUP, :] = block40[:, m * LANES : (m + 1) * LANES]
    for j in range(ZN):
        for m in range(5):
            part = tiles[m, pl.ds(j, COLS, stride=ZN), :]
            fs_f[j, m * COLS : (m + 1) * COLS, :] = part
    fs[...] = fs_f[...].astype(BF)

    def f_copy(k):
        to = (z + k) % ZN
        return rcopy(fs.at[to], fs_land.at[k], f_s.at[k], f_r.at[k], dpi(to, xx), s)

    for k in (4, 3, 5, 2, 6, 1, 7):
        f_copy(k).start()
    final = fs_f[z]
    for k in range(1, ZN):
        f_copy(k).wait_recv()
        final = final + fs_land[k].astype(F32)
    fs_f[0] = final
    for m in range(COLS):
        og_ref[:, m * LANES : (m + 1) * LANES] = fs_f[0, m * COLS : (m + 1) * COLS, :]

    for k in range(1, SEQ):
        x_copy(k, s).wait_send()
        a_copy(0, s, k).wait_send()
    for k in range(1, ZN):
        w1_copy(k, z).wait_send()
        f_copy(k).wait_send()
    for k in range(1, XN):
        w2_copy(k, None).wait_send()
        w3_copy(k, s).wait_send()
        ya_copy(k).wait_send()
        for j in range(YN):
            xb_copy(k, j).wait_send()
        ax_copy(k).wait_send()
        by_copy(k).wait_send()
    for k in range(YN):
        w4_copy(k, c).wait_send()
        m_copy(k, c).wait_send()
        p_copy(k).wait_send()


def hand_over(lo_in, og_in, lo_out, og_out, sem):
    copies = [pltpu.make_async_copy(og_in, og_out, sem.at[0])]
    for j in range(4):
        rows = pl.ds(j * 96, 96)
        copies.append(pltpu.make_async_copy(lo_in.at[rows, :], lo_out.at[rows, :], sem.at[j + 1]))
    for copy in copies:
        copy.start()
    for copy in copies:
        copy.wait()


def per_device(
    patches,
    segment_ids,
    regroup_plan,
    input_weight,
    input_bias,
    skip_weight,
    hidden_weight,
    output_bias,
    norm_gain,
    head_scale,
    qkv_weight,
    out_weight,
    cotangent,
):
    vmem = pl.BlockSpec(memory_space=pltpu.VMEM)
    hbm = pl.BlockSpec(memory_space=pltpu.HBM)
    dma = pltpu.SemaphoreType.DMA
    scratch = [
        pltpu.VMEM((1, WIN), jnp.int32),
        pltpu.VMEM((5, 1, 64), jnp.int32),
        pltpu.VMEM((PATCH, D), BF),
        pltpu.VMEM((D,), F32),
        pltpu.VMEM((PATCH, D), BF),
        pltpu.VMEM((D,), F32),
        pltpu.VMEM((D,), F32),
        pltpu.SMEM((SEQ,), F32),
        pltpu.VMEM((COLS, HW), BF),
        pltpu.VMEM((D, D), BF),
        pltpu.VMEM((3, D, 2 * LANES), BF),
        pltpu.VMEM((ROWS, D), BF),
        pltpu.VMEM((3, D, LANES), F32),
        pltpu.VMEM((2, HW, ROWS), BF),
        pltpu.VMEM((SEQ * PATCH, ROWS), BF),
        pltpu.VMEM((SEQ * PATCH, D), BF),
        pltpu.VMEM((SEQ * PATCH, D), BF),
        pltpu.VMEM((D, 6 * LANES), BF),
        pltpu.VMEM((WIN, 3 * LANES), BF),
        pltpu.VMEM((4, ROWS, 3 * LANES), BF),
        pltpu.VMEM((4, ROWS, D), BF),
        pltpu.VMEM((8, HW), F32),
        pltpu.VMEM((ZN * 8, HW), F32),
        pltpu.VMEM((XN, 48, HW), BF),
        pltpu.VMEM((D, HW), BF),
        pltpu.VMEM((5, D, LANES), F32),
        pltpu.VMEM((5, 64, LANES), F32),
        pltpu.VMEM((SEQ, HD, ROWS), BF),
        pltpu.VMEM((HW, ROWS), BF),
        pltpu.VMEM((HW, HW), F32),
        pltpu.VMEM((YN, 160, HW), BF),
        pltpu.VMEM((YN, 160, HW), BF),
        pltpu.VMEM((YN, 160, ROWS), BF),
        pltpu.VMEM((YN, 160, ROWS), BF),
        pltpu.VMEM((XN, YN, 48, HW - ROWS), BF),
        pltpu.VMEM((XN, YN, 48, HW - ROWS), BF),
        pltpu.VMEM((XN, 48, ROWS), BF),
        pltpu.VMEM((XN, 48, ROWS), BF),
        pltpu.VMEM((YN, 48, HW - ROWS), BF),
        pltpu.VMEM((YN, 48, HW - ROWS), BF),
        pltpu.VMEM((GROUP, HW), F32),
        pltpu.VMEM((ZN, 32, LANES), F32),
        pltpu.VMEM((ZN, 32, LANES), BF),
        pltpu.VMEM((ZN, 32, LANES), BF),
        dma((13,)),
        dma((8,)),
        dma((8,)),
        dma((8,)),
        dma((8,)),
        dma((4,)),
        dma((4,)),
        dma((4,)),
        dma((4,)),
        dma((4,)),
        dma((4,)),
        dma((4,)),
        dma((4,)),
        dma((8,)),
        dma((8,)),
        dma((4,)),
        dma((4,)),
        dma((4,)),
        dma((4,)),
        dma((16,)),
        dma((16,)),
        dma((4,)),
        dma((4,)),
        dma((4,)),
        dma((4,)),
        dma((8,)),
        dma((8,)),
    ]
    layer_out, grad = pl.pallas_call(
        whole_layer,
        out_shape=(
            jax.ShapeDtypeStruct((ROWS, D), BF),
            jax.ShapeDtypeStruct((COLS, HW), F32),
        ),
        in_specs=[hbm] * 13,
        out_specs=(vmem, vmem),
        scratch_shapes=scratch,
        compiler_params=pltpu.CompilerParams(
            collective_id=0, has_side_effects=True, vmem_limit_bytes=63 * 1024 * 1024
        ),
        name="whole_layer",
    )(
        patches,
        segment_ids,
        jnp.transpose(regroup_plan, (1, 0, 2)),
        input_weight,
        input_bias,
        skip_weight,
        hidden_weight,
        output_bias,
        norm_gain,
        head_scale,
        jnp.transpose(qkv_weight, (1, 0, 2)),
        jnp.transpose(out_weight),
        cotangent,
    )
    layer_out, grad = pl.pallas_call(
        hand_over,
        out_shape=(
            jax.ShapeDtypeStruct((ROWS, D), BF),
            jax.ShapeDtypeStruct((COLS, HW), F32),
        ),
        in_specs=[hbm, hbm],
        out_specs=(hbm, hbm),
        scratch_shapes=[dma((5,))],
        name="hand_over",
    )(layer_out, grad)
    return layer_out, jnp.transpose(grad)


def solution(mesh):
    placed = (
        P(None, ("dp", "seq")),
        P("dp", None),
        P("dp", None, None),
        P(),
        P(),
        P(),
        P(),
        P(),
        P(),
        P(),
        P(),
        P(None, ("dp", "seq")),
        P(("dp", "seq"), None),
    )
    return jax.shard_map(
        per_device,
        mesh=mesh,
        in_specs=placed,
        out_specs=(P(("dp", "seq"), None), P(None, ("dp", "seq"))),
        check_vma=False,
    )
```

```python
import functools
import math

import jax
import jax.numpy as jnp
from jax import lax
from jax.experimental import pallas as pl
from jax.experimental.pallas import tpu as pltpu
from jax.sharding import PartitionSpec as P

HD = 80
LANES = 128
ZN, XN, YN = 8, 4, 4
SEQ = 8
ROWS = 384
WIN = ROWS * SEQ
D = 1280
HW = 640
PATCH = 32
COLS = 5
GROUP = COLS * SEQ
EPS = 1e-06
MASKED = 2048.0
LOG2E = 1.4426950408889634
MESH = pl.DeviceIdType.MESH
BF = jnp.bfloat16
F32 = jnp.float32
NT = (((1,), (1,)), ((), ()))


def iota(shape, dim):
    return lax.broadcasted_iota(jnp.int32, shape, dim)


def dot(a, b):
    return jnp.dot(a, b, preferred_element_type=F32)


def dot_nt(a, b):
    return lax.dot_general(a, b, NT, preferred_element_type=F32)


def whole_layer(
    x_hbm,
    seg_hbm,
    plan_hbm,
    win_hbm,
    bin_hbm,
    wskip_hbm,
    wh_hbm,
    ob_hbm,
    gain_hbm,
    hs_hbm,
    qkvw_hbm,
    ow_hbm,
    cot_hbm,
    lo_ref,
    og_ref,
    seg_ref,
    plan_ref,
    win_ref,
    bin_ref,
    wskip_ref,
    ob_ref,
    gain_ref,
    hs_ref,
    ow_ref,
    wh,
    qkvw,
    cot,
    cot_f,
    cot_t,
    xg,
    win8,
    wskip8,
    wsel,
    qkv,
    msend,
    emb_own,
    ow_send,
    w_land,
    wx,
    wt,
    wt_f,
    tiles,
    att_send,
    ret,
    p_own,
    p_send,
    p_land,
    ya,
    ya_land,
    xb,
    xb_land,
    ax,
    ax_land,
    by,
    by_land,
    block40,
    fs_f,
    fs,
    fs_land,
    ld_sem,
    x_s,
    x_r,
    w1_s,
    w1_r,
    w2_s,
    w2_r,
    w3_s,
    w3_r,
    w4_s,
    w4_r,
    m_s,
    m_r,
    a_s,
    a_r,
    p_s,
    p_r,
    ya_s,
    ya_r,
    xb_s,
    xb_r,
    ax_s,
    ax_r,
    by_s,
    by_r,
    f_s,
    f_r,
):
    dp = lax.axis_index("dp")
    s = lax.axis_index("seq")
    z = dp // XN
    xx = dp % XN
    y = s // 2
    c = s % 2
    mate = y * 2 + (1 - c)
    def rcopy(src, dst, ssem, rsem, dp_t, seq_t):
        return pltpu.make_async_remote_copy(
            src_ref=src,
            dst_ref=dst,
            send_sem=ssem,
            recv_sem=rsem,
            device_id=(dp_t, seq_t),
            device_id_type=MESH,
        )

    def dpi(zz, x2):
        return zz * XN + x2

    bar = pltpu.get_barrier_semaphore()

    def greet(dp_t, seq_t):
        pl.semaphore_signal(bar, inc=1, device_id=(dp_t, seq_t), device_id_type=MESH)

    for k in range(1, SEQ):
        greet(dp, (s + k) % SEQ)
    for k in range(1, XN):
        greet(dpi(z, (xx + k) % XN), s)
    for k in range(1, ZN):
        greet(dpi((z + k) % ZN, xx), s)

    loads = [
        pltpu.make_async_copy(src, dst, ld_sem.at[i])
        for i, (src, dst) in enumerate(
            [
                (x_hbm, xg.at[pl.ds(pl.multiple_of(s * PATCH, PATCH), PATCH), :]),
                (ow_hbm, ow_ref),
                (win_hbm, win_ref),
                (wskip_hbm, wskip_ref),
                (qkvw_hbm.at[:, :, pl.ds(pl.multiple_of(y * LANES, LANES), 2 * LANES)], qkvw),
                (plan_hbm, plan_ref),
                (seg_hbm, seg_ref),
                (bin_hbm, bin_ref),
                (ob_hbm, ob_ref),
                (gain_hbm, gain_ref),
                (hs_hbm, hs_ref),
                (wh_hbm, wh),
                (cot_hbm, cot),
            ]
        )
    ]
    for ld in loads:
        ld.start()

    pl.semaphore_wait(bar, 7 + 3 + 7)

    def x_copy(k, source):
        rows = xg.at[pl.ds(pl.multiple_of(source * PATCH, PATCH), PATCH), :]
        return rcopy(x_hbm, rows, x_s.at[k], x_r.at[k], dp, (s + k) % SEQ)

    for k in range(1, SEQ):
        x_copy(k, s).start()

    for ld in loads[1:2]:
        ld.wait()
    ow_send[...] = jnp.zeros((8, HW), F32)
    ow_send[0:COLS, :] = ow_ref[...].astype(F32)

    def w1_copy(k, source):
        slot = w_land.at[pl.ds(pl.multiple_of(source * 8, 8), 8), :]
        return rcopy(ow_send, slot, w1_s.at[k], w1_r.at[k], dpi((z + k) % ZN, xx), s)

    for k in range(1, ZN):
        w1_copy(k, z).start()
    w_land[pl.ds(pl.multiple_of(z * 8, 8), 8), :] = ow_send[...]

    for ld in (loads[0], *loads[2:4]):
        ld.wait()
    for k in range(SEQ):
        win8[k * PATCH : (k + 1) * PATCH, :] = win_ref[...]
        wskip8[k * PATCH : (k + 1) * PATCH, :] = wskip_ref[...]

    loads[4].wait()
    feature = iota((2 * LANES, 2 * LANES), 0) + y * LANES
    lane2 = iota((2 * LANES, 2 * LANES), 1)
    inner = lane2 % LANES
    head = jnp.where(lane2 < LANES, s, mate)
    pick = jnp.where((inner < HD) & (feature == head * HD + inner), 1.0, 0.0).astype(BF)
    for i in range(3):
        part = dot(qkvw[i], pick).astype(BF)
        wsel[:, i * LANES : (i + 1) * LANES] = part[:, :LANES]
        wsel[:, (3 + i) * LANES : (4 + i) * LANES] = part[:, LANES:]
    for ld in loads[5:12]:
        ld.wait()
    for k in range(1, SEQ):
        x_copy(k, (s - k + SEQ) % SEQ).wait_recv()

    def w2_copy(k, source):
        return rcopy(
            wx.at[xx] if source is None else wx.at[xx],
            wx.at[xx if source is None else source],
            w2_s.at[k],
            w2_r.at[k],
            dpi(z, (xx + k) % XN),
            s,
        )

    def wt_rows(zz):
        return wt.at[pl.ds(pl.multiple_of(zz * 160, 32), 160), :]

    def w3_copy(k, source):
        block = wt_rows(source)
        return rcopy(block, block, w3_s.at[k], w3_r.at[k], dp, ((y + k) % YN) * 2 + c)

    def w4_copy(k, core):
        block = wt_rows(((y - k + YN) % YN) * 2 + core)
        return rcopy(block, block, w4_s.at[k], w4_r.at[k], dp, mate)

    def m_copy(i, core):
        rows = pl.multiple_of((2 * i + core) * ROWS, ROWS)
        return rcopy(msend.at[i], qkv.at[pl.ds(rows, ROWS), :], m_s.at[i], m_r.at[i], dp, mate)

    lane = iota((2 * ROWS, LANES), 1)
    seg_lane = (lane >= HD) & (lane < HD + 16)

    def embed_rows(g):
        begin = [pl.multiple_of((4 * g + 2 * e + c) * ROWS, ROWS) for e in range(2)]
        step = iota((2 * ROWS, 64), 0)
        pos = begin[0] + step + jnp.where(step >= ROWS, ROWS, 0)
        source, first, count = plan_ref[0], plan_ref[1], plan_ref[2]
        start = plan_ref[3] * ROWS + plan_ref[4]
        inside = (pos >= start) & (pos < start + count)
        code = jnp.where(inside, (source * 512 + first - start) + pos, 0)
        code = jnp.sum(code.astype(F32), axis=1, keepdims=True).astype(jnp.int32)
        row_of = code % 512
        shard_of = code // 512
        onehot = jnp.where(iota((2 * ROWS, ROWS), 1) == row_of, 1.0, 0.0).astype(BF)
        spread = dot_nt(onehot, xg[...])
        cols = jnp.where(
            iota((2 * ROWS, SEQ * PATCH), 1) // PATCH == shard_of, spread, 0.0
        ).astype(BF)
        half = (dot(cols, win8[...]) + bin_ref[...].reshape(1, D)) * 0.5
        hidden = (half + half * jnp.tanh(half)).astype(BF)
        emb = dot(hidden, wh[...]) + dot(cols, wskip8[...]) + ob_ref[...].reshape(1, D)
        emb = emb.astype(BF)
        emb_own[2 * g] = emb[:ROWS]
        emb_own[2 * g + 1] = emb[ROWS:]
        return begin, emb

    def project_rows(g, begin, emb):
        wide = emb.astype(F32)
        scale = lax.rsqrt(jnp.mean(wide * wide, axis=-1, keepdims=True) + EPS)
        normed = (wide * scale * gain_ref[...].reshape(1, D)).astype(BF)
        proj = dot(normed, wsel[...]).astype(BF)

        marks = []
        for e in range(2):
            seg_row = seg_ref[:, pl.ds(begin[e], ROWS)]
            match = jnp.where(iota((LANES, ROWS), 0) - HD == seg_row, 1.0, 0.0)
            marks.append(jnp.transpose(match))
        marks = jnp.concatenate(marks, axis=0)
        away = jnp.where(seg_lane, (marks - 1.0) * MASKED, 0.0)
        ones = jnp.where(lane == HD, 1.0, 0.0)
        for h in (1, 0):
            q = proj[:, (3 * h) * LANES : (3 * h + 1) * LANES].astype(F32)
            k = proj[:, (3 * h + 1) * LANES : (3 * h + 2) * LANES].astype(F32)
            v = proj[:, (3 * h + 2) * LANES : (3 * h + 3) * LANES].astype(F32)
            q = q * lax.rsqrt(jnp.sum(q * q, axis=-1, keepdims=True) * (1.0 / HD) + EPS)
            k = k * lax.rsqrt(jnp.sum(k * k, axis=-1, keepdims=True) * (1.0 / HD) + EPS)
            parts = [(q + away).astype(BF), (k + marks).astype(BF), (v + ones).astype(BF)]
            for e in range(2):
                for j in range(3):
                    part = parts[j][e * ROWS : (e + 1) * ROWS]
                    lanes = slice(j * LANES, (j + 1) * LANES)
                    if h:
                        msend[2 * g + e, :, lanes] = part
                    else:
                        qkv[pl.ds(begin[e], ROWS), lanes] = part
            if h:
                m_copy(2 * g, c).start()
                m_copy(2 * g + 1, c).start()

    begin, emb = embed_rows(0)
    for k in range(1, ZN):
        w1_copy(k, (z - k + ZN) % ZN).wait_recv()
    for m in range(5):
        tiles[m] = w_land[:, m * LANES : (m + 1) * LANES]
    block = jnp.concatenate(
        [
            jnp.concatenate([tiles[m, pl.ds(j, ZN, stride=8), :] for j in range(COLS)], axis=0)
            for m in range(5)
        ],
        axis=1,
    )
    block = jnp.concatenate([block, jnp.zeros((8, HW), F32)], axis=0)
    wx[xx] = block.astype(BF)
    for k in range(1, XN):
        w2_copy(k, None).start()
    project_rows(0, begin, emb)
    for k in range(1, XN):
        w2_copy(k, (xx - k + XN) % XN).wait_recv()
    block = jnp.concatenate([wx[j, 0:GROUP, :].astype(F32) for j in range(XN)], axis=0)
    wt[pl.ds(pl.multiple_of(s * 160, 32), 160), :] = block.astype(BF)
    for k in range(1, YN):
        w3_copy(k, s).start()
    w4_copy(0, c).start()
    project_rows(1, *embed_rows(1))
    factor = hs_ref[s] * (LOG2E / math.sqrt(HD))
    causal = iota((ROWS, ROWS), 0) >= iota((ROWS, ROWS), 1)

    def a_copy(block, source, k):
        rows = ret.at[pl.ds(pl.multiple_of(source * HD, 16), HD), :]
        return rcopy(att_send.at[block], rows, a_s.at[k], a_r.at[k], dp, (s + k) % SEQ)

    for i in range(2):
        m_copy(i, 1 - c).wait_recv()
    for b in (3, 2, 7, 0, 5, 1, 6, 4):
        if b == 7:
            for i in range(2, 4):
                m_copy(i, 1 - c).wait_recv()
        q = qkv[b * ROWS : (b + 1) * ROWS, 0:LANES]
        total = jnp.zeros((ROWS, LANES), F32)
        edges = list(range(0, b * ROWS, 2 * ROWS)) + [b * ROWS]
        for lo, hi in zip(edges[:-1], edges[1:]):
            scores = dot_nt(q, qkv[lo:hi, LANES : 2 * LANES]) * factor
            total = total + dot(jnp.exp2(scores).astype(BF), qkv[lo:hi, 2 * LANES : 3 * LANES])
        lo, hi = b * ROWS, (b + 1) * ROWS
        scores = dot_nt(q, qkv[lo:hi, LANES : 2 * LANES]) * factor
        weights = jnp.where(causal, jnp.exp2(scores), 0.0).astype(BF)
        total = total + dot(weights, qkv[lo:hi, 2 * LANES : 3 * LANES])
        across = jnp.transpose(total)
        out = (across[0:HD, :] / across[HD : HD + 1, :]).astype(BF)
        att_send[b] = out

        @pl.when(s == b)
        def _():
            ret[pl.ds(pl.multiple_of(s * HD, 16), HD), :] = out

        @pl.when(s != b)
        def _():
            a_copy(b, s, (b - s + SEQ) % SEQ).start()

        if b == 5:
            for k in range(1, YN):
                w3_copy(k, ((y - k + YN) % YN) * 2 + c).wait_recv()
                w4_copy(k, c).start()

    loads[12].wait()
    for m in range(3):
        cot_f[m] = jnp.transpose(cot[m * LANES : (m + 1) * LANES, :].astype(F32))
    for core in range(2):
        for j in range(YN):
            base = [x2 * GROUP + (2 * j + core) * COLS + n for x2 in range(XN) for n in range(COLS)]
            for m in range(3):
                rows = [cot_f[m, pl.ds(first, ZN, stride=160), :] for first in base]
                rows = jnp.concatenate(rows, axis=0).astype(BF)
                cot_t[core, j * 160 : (j + 1) * 160, m * LANES : (m + 1) * LANES] = rows
    for k in range(YN):
        w4_copy(k, 1 - c).wait_recv()
    for t in range(SEQ):
        block = wt[t * 160 : (t + 1) * 160, :].astype(F32)
        for x2 in range(XN):
            for n in range(COLS):
                first = x2 * GROUP + n * ZN
                rows = pl.ds(x2 * GROUP + t * COLS + n, ZN, stride=160)
                for m in range(5):
                    wt_f[m, rows, :] = block[first : first + ZN, m * LANES : (m + 1) * LANES]

    for k in range(1, SEQ):
        a_copy(0, (s - k + SEQ) % SEQ, k).wait_recv()

    attended = ret[...]
    order = [2, 1, 3, 0]

    def p_copy(k):
        piece = (y + k) % YN
        return rcopy(p_send.at[piece], p_land.at[piece], p_s.at[k], p_r.at[k], dp, mate)

    def owner_rows(k):
        return pl.ds(pl.multiple_of(((y + k) % YN) * 160, 32), 160)

    for k in order:
        p_send[(y + k) % YN] = dot_nt(cot_t[1 - c, owner_rows(k), :], attended).astype(BF)
        p_copy(k).start()
    p_own[...] = dot_nt(cot_t[c], attended)

    def ya_copy(k):
        to = (y + k) % YN
        return rcopy(ya.at[to], ya_land.at[k], ya_s.at[k], ya_r.at[k], dp, to * 2 + c)

    def xb_copy(k, row):
        to = (xx + k) % XN
        slot = k * YN + row
        return rcopy(
            xb.at[to, row], xb_land.at[k, row], xb_s.at[slot], xb_r.at[slot], dpi(z, to), s
        )

    pad = jnp.zeros((8, HW - ROWS), F32)
    for k in order:
        to = (y + k) % YN
        p_copy(k).wait_recv()
        piece = p_own[owner_rows(k), :] + p_land[to].astype(F32)
        p_own[owner_rows(k), :] = piece
        if k:
            ya[to] = piece[:, 0:ROWS].astype(BF)
            ya_copy(k).start()
        for j in range(XN):
            part = piece[j * GROUP : (j + 1) * GROUP, ROWS:]
            xb[j, to] = jnp.concatenate([part, pad], axis=0).astype(BF)
        for j in (2, 1, 3):
            xb_copy(j, to).start()

    rows = jnp.transpose(attended)
    for j in range(5):
        cols = slice(j * 256, (j + 1) * 256)
        weight = jnp.concatenate([wt_f[m, cols, :].astype(BF) for m in range(5)], axis=1)
        branch = dot_nt(rows, weight)
        lo_ref[:, cols] = (emb_own[y, :, cols].astype(F32) + branch).astype(BF)

    for k in range(1, YN):
        ya_copy(k).wait_recv()
    own = p_own[pl.ds(pl.multiple_of(y * 160, 32), 160), :]
    a_sum = own[:, 0:ROWS]
    for k in range(1, YN):
        a_sum = a_sum + ya_land[k].astype(F32)
    pad = jnp.zeros((8, ROWS), F32)
    block40[...] = jnp.zeros_like(block40)
    for j in range(XN):
        piece = a_sum[j * GROUP : (j + 1) * GROUP, :]
        ax[j] = jnp.concatenate([piece, pad], axis=0).astype(BF)

        @pl.when(xx == j)
        def _():
            block40[:, 0:ROWS] = piece

    def ax_copy(k):
        to = (xx + k) % XN
        return rcopy(ax.at[to], ax_land.at[k], ax_s.at[k], ax_r.at[k], dpi(z, to), s)

    for k in range(1, XN):
        ax_copy(k).start()

    for k in range(1, XN):
        for j in range(YN):
            xb_copy(k, j).wait_recv()
    pad = jnp.zeros((8, HW - ROWS), F32)
    for j in range(YN):
        begin = pl.multiple_of((j * XN + xx) * GROUP, 8)
        piece = p_own[pl.ds(begin, GROUP), ROWS:HW]
        for k in range(1, XN):
            piece = piece + xb_land[k, j].astype(F32)[0:GROUP, :]
        by[j] = jnp.concatenate([piece, pad], axis=0).astype(BF)

        @pl.when(y == j)
        def _():
            block40[:, ROWS:HW] = piece

    def by_copy(k):
        to = (y + k) % YN
        return rcopy(by.at[to], by_land.at[k], by_s.at[k], by_r.at[k], dp, to * 2 + c)

    for k in range(1, YN):
        by_copy(k).start()
    for k in range(1, XN):
        ax_copy(k).wait_recv()
    for k in range(1, YN):
        by_copy(k).wait_recv()
    left = block40[:, 0:ROWS]
    right = block40[:, ROWS:HW]
    for k in range(1, XN):
        left = left + ax_land[k].astype(F32)[0:GROUP, :]
        right = right + by_land[k].astype(F32)[0:GROUP, :]
    block40[:, 0:ROWS] = left
    block40[:, ROWS:HW] = right
    for m in range(5):
        tiles[m, 0:GROUP, :] = block40[:, m * LANES : (m + 1) * LANES]
    for j in range(ZN):
        for m in range(5):
            part = tiles[m, pl.ds(j, COLS, stride=ZN), :]
            fs_f[j, m * COLS : (m + 1) * COLS, :] = part
    fs[...] = fs_f[...].astype(BF)

    def f_copy(k):
        to = (z + k) % ZN
        return rcopy(fs.at[to], fs_land.at[k], f_s.at[k], f_r.at[k], dpi(to, xx), s)

    for k in (4, 3, 5, 2, 6, 1, 7):
        f_copy(k).start()
    final = fs_f[z]
    for k in range(1, ZN):
        f_copy(k).wait_recv()
        final = final + fs_land[k].astype(F32)
    fs_f[0] = final
    for m in range(COLS):
        og_ref[:, m * LANES : (m + 1) * LANES] = fs_f[0, m * COLS : (m + 1) * COLS, :]

    for k in range(1, SEQ):
        x_copy(k, s).wait_send()
        a_copy(0, s, k).wait_send()
    for k in range(1, ZN):
        w1_copy(k, z).wait_send()
        f_copy(k).wait_send()
    for k in range(1, XN):
        w2_copy(k, None).wait_send()
        w3_copy(k, s).wait_send()
        ya_copy(k).wait_send()
        for j in range(YN):
            xb_copy(k, j).wait_send()
        ax_copy(k).wait_send()
        by_copy(k).wait_send()
    for k in range(YN):
        w4_copy(k, c).wait_send()
        m_copy(k, c).wait_send()
        p_copy(k).wait_send()


def hand_over(lo_in, og_in, lo_out, og_out, lo_vmem, og_vmem, sem_in, sem_out):
    def parts(lo, og):
        rows = [pl.ds(k * 128, 128) for k in range(3)]
        return [lo.at[r, :] for r in rows] + [og]

    held = parts(lo_vmem, og_vmem)
    into = [
        pltpu.make_async_copy(a, b, sem_in.at[k])
        for k, (a, b) in enumerate(zip(parts(lo_in, og_in), held))
    ]
    back = [
        pltpu.make_async_copy(a, b, sem_out.at[k])
        for k, (a, b) in enumerate(zip(held, parts(lo_out, og_out)))
    ]
    for copy in into:
        copy.start()
    for a, b in zip(into, back):
        a.wait()
        b.start()
    for copy in back:
        copy.wait()


def per_device(
    patches,
    segment_ids,
    regroup_plan,
    input_weight,
    input_bias,
    skip_weight,
    hidden_weight,
    output_bias,
    norm_gain,
    head_scale,
    qkv_weight,
    out_weight,
    cotangent,
):
    vmem = pl.BlockSpec(memory_space=pltpu.VMEM)
    hbm = pl.BlockSpec(memory_space=pltpu.HBM)
    dma = pltpu.SemaphoreType.DMA
    scratch = [
        pltpu.VMEM((1, WIN), jnp.int32),
        pltpu.VMEM((5, 1, 64), jnp.int32),
        pltpu.VMEM((PATCH, D), BF),
        pltpu.VMEM((D,), F32),
        pltpu.VMEM((PATCH, D), BF),
        pltpu.VMEM((D,), F32),
        pltpu.VMEM((D,), F32),
        pltpu.SMEM((SEQ,), F32),
        pltpu.VMEM((COLS, HW), BF),
        pltpu.VMEM((D, D), BF),
        pltpu.VMEM((3, D, 2 * LANES), BF),
        pltpu.VMEM((ROWS, D), BF),
        pltpu.VMEM((3, D, LANES), F32),
        pltpu.VMEM((2, HW, ROWS), BF),
        pltpu.VMEM((SEQ * PATCH, ROWS), BF),
        pltpu.VMEM((SEQ * PATCH, D), BF),
        pltpu.VMEM((SEQ * PATCH, D), BF),
        pltpu.VMEM((D, 6 * LANES), BF),
        pltpu.VMEM((WIN, 3 * LANES), BF),
        pltpu.VMEM((4, ROWS, 3 * LANES), BF),
        pltpu.VMEM((4, ROWS, D), BF),
        pltpu.VMEM((8, HW), F32),
        pltpu.VMEM((ZN * 8, HW), F32),
        pltpu.VMEM((XN, 48, HW), BF),
        pltpu.VMEM((D, HW), BF),
        pltpu.VMEM((5, D, LANES), F32),
        pltpu.VMEM((5, 64, LANES), F32),
        pltpu.VMEM((SEQ, HD, ROWS), BF),
        pltpu.VMEM((HW, ROWS), BF),
        pltpu.VMEM((HW, HW), F32),
        pltpu.VMEM((YN, 160, HW), BF),
        pltpu.VMEM((YN, 160, HW), BF),
        pltpu.VMEM((YN, 160, ROWS), BF),
        pltpu.VMEM((YN, 160, ROWS), BF),
        pltpu.VMEM((XN, YN, 48, HW - ROWS), BF),
        pltpu.VMEM((XN, YN, 48, HW - ROWS), BF),
        pltpu.VMEM((XN, 48, ROWS), BF),
        pltpu.VMEM((XN, 48, ROWS), BF),
        pltpu.VMEM((YN, 48, HW - ROWS), BF),
        pltpu.VMEM((YN, 48, HW - ROWS), BF),
        pltpu.VMEM((GROUP, HW), F32),
        pltpu.VMEM((ZN, 32, LANES), F32),
        pltpu.VMEM((ZN, 32, LANES), BF),
        pltpu.VMEM((ZN, 32, LANES), BF),
        dma((13,)),
        dma((8,)),
        dma((8,)),
        dma((8,)),
        dma((8,)),
        dma((4,)),
        dma((4,)),
        dma((4,)),
        dma((4,)),
        dma((4,)),
        dma((4,)),
        dma((4,)),
        dma((4,)),
        dma((8,)),
        dma((8,)),
        dma((4,)),
        dma((4,)),
        dma((4,)),
        dma((4,)),
        dma((16,)),
        dma((16,)),
        dma((4,)),
        dma((4,)),
        dma((4,)),
        dma((4,)),
        dma((8,)),
        dma((8,)),
    ]
    layer_out, grad = pl.pallas_call(
        whole_layer,
        out_shape=(
            jax.ShapeDtypeStruct((ROWS, D), BF),
            jax.ShapeDtypeStruct((COLS, HW), F32),
        ),
        in_specs=[hbm] * 13,
        out_specs=(vmem, vmem),
        scratch_shapes=scratch,
        compiler_params=pltpu.CompilerParams(
            collective_id=0, has_side_effects=True, vmem_limit_bytes=63 * 1024 * 1024
        ),
        name="whole_layer",
    )(
        patches,
        segment_ids,
        jnp.transpose(regroup_plan, (1, 0, 2)),
        input_weight,
        input_bias,
        skip_weight,
        hidden_weight,
        output_bias,
        norm_gain,
        head_scale,
        jnp.transpose(qkv_weight, (1, 0, 2)),
        jnp.transpose(out_weight),
        cotangent,
    )
    layer_out, grad = pl.pallas_call(
        hand_over,
        out_shape=(
            jax.ShapeDtypeStruct((ROWS, D), BF),
            jax.ShapeDtypeStruct((COLS, HW), F32),
        ),
        in_specs=[hbm, hbm],
        out_specs=(hbm, hbm),
        scratch_shapes=[
            pltpu.VMEM((ROWS, D), BF),
            pltpu.VMEM((COLS, HW), F32),
            dma((4,)),
            dma((4,)),
        ],
        name="hand_over",
    )(layer_out, grad)
    return layer_out, jnp.transpose(grad)


def solution(mesh):
    placed = (
        P(None, ("dp", "seq")),
        P("dp", None),
        P("dp", None, None),
        P(),
        P(),
        P(),
        P(),
        P(),
        P(),
        P(),
        P(),
        P(None, ("dp", "seq")),
        P(("dp", "seq"), None),
    )
    return jax.shard_map(
        per_device,
        mesh=mesh,
        in_specs=placed,
        out_specs=(P(("dp", "seq"), None), P(None, ("dp", "seq"))),
        check_vma=False,
    )
```

```python
import functools
import math

import jax
import jax.numpy as jnp
from jax import lax
from jax.experimental import pallas as pl
from jax.experimental.pallas import tpu as pltpu
from jax.sharding import PartitionSpec as P

HD = 80
LANES = 128
ZN, XN, YN = 8, 4, 4
SEQ = 8
ROWS = 384
WIN = ROWS * SEQ
D = 1280
HW = 640
PATCH = 32
COLS = 5
GROUP = COLS * SEQ
EPS = 1e-06
MASKED = 2048.0
LOG2E = 1.4426950408889634
MESH = pl.DeviceIdType.MESH
BF = jnp.bfloat16
F32 = jnp.float32
NT = (((1,), (1,)), ((), ()))


def iota(shape, dim):
    return lax.broadcasted_iota(jnp.int32, shape, dim)


def dot(a, b):
    return jnp.dot(a, b, preferred_element_type=F32)


def dot_nt(a, b):
    return lax.dot_general(a, b, NT, preferred_element_type=F32)


def whole_layer(
    x_hbm,
    seg_hbm,
    plan_hbm,
    win_hbm,
    bin_hbm,
    wskip_hbm,
    wh_hbm,
    ob_hbm,
    gain_hbm,
    hs_hbm,
    qkvw_hbm,
    ow_hbm,
    cot_hbm,
    lo_ref,
    og_ref,
    seg_ref,
    plan_ref,
    win_ref,
    bin_ref,
    wskip_ref,
    ob_ref,
    gain_ref,
    hs_ref,
    ow_ref,
    wh,
    qkvw,
    cot,
    cot_f,
    cot_t,
    xg,
    win8,
    wskip8,
    wsel,
    qkv,
    msend,
    emb_own,
    ow_send,
    w_land,
    wx,
    wt,
    wt_f,
    tiles,
    att_send,
    ret,
    p_own,
    cot_m,
    ya,
    ya_land,
    xb,
    xb_land,
    ax,
    ax_land,
    by,
    by_land,
    block40,
    fs_f,
    fs,
    fs_land,
    ld_sem,
    x_s,
    x_r,
    w1_s,
    w1_r,
    w2_s,
    w2_r,
    w3_s,
    w3_r,
    w4_s,
    w4_r,
    m_s,
    m_r,
    a_s,
    a_r,
    p_s,
    p_r,
    c_s,
    c_r,
    ya_s,
    ya_r,
    xb_s,
    xb_r,
    ax_s,
    ax_r,
    by_s,
    by_r,
    f_s,
    f_r,
):
    dp = lax.axis_index("dp")
    s = lax.axis_index("seq")
    z = dp // XN
    xx = dp % XN
    y = s // 2
    c = s % 2
    mate = y * 2 + (1 - c)
    def rcopy(src, dst, ssem, rsem, dp_t, seq_t):
        return pltpu.make_async_remote_copy(
            src_ref=src,
            dst_ref=dst,
            send_sem=ssem,
            recv_sem=rsem,
            device_id=(dp_t, seq_t),
            device_id_type=MESH,
        )

    def dpi(zz, x2):
        return zz * XN + x2

    bar = pltpu.get_barrier_semaphore()

    def greet(dp_t, seq_t):
        pl.semaphore_signal(bar, inc=1, device_id=(dp_t, seq_t), device_id_type=MESH)

    for k in range(1, SEQ):
        greet(dp, (s + k) % SEQ)
    for k in range(1, XN):
        greet(dpi(z, (xx + k) % XN), s)
    for k in range(1, ZN):
        greet(dpi((z + k) % ZN, xx), s)

    loads = [
        pltpu.make_async_copy(src, dst, ld_sem.at[i])
        for i, (src, dst) in enumerate(
            [
                (x_hbm, xg.at[pl.ds(pl.multiple_of(s * PATCH, PATCH), PATCH), :]),
                (ow_hbm, ow_ref),
                (win_hbm, win_ref),
                (wskip_hbm, wskip_ref),
                (qkvw_hbm.at[:, :, pl.ds(pl.multiple_of(y * LANES, LANES), 2 * LANES)], qkvw),
                (plan_hbm, plan_ref),
                (seg_hbm, seg_ref),
                (bin_hbm, bin_ref),
                (ob_hbm, ob_ref),
                (gain_hbm, gain_ref),
                (hs_hbm, hs_ref),
                (wh_hbm, wh),
                (cot_hbm, cot),
            ]
        )
    ]
    for ld in loads:
        ld.start()

    pl.semaphore_wait(bar, 7 + 3 + 7)

    def x_copy(k, source):
        rows = xg.at[pl.ds(pl.multiple_of(source * PATCH, PATCH), PATCH), :]
        return rcopy(x_hbm, rows, x_s.at[k], x_r.at[k], dp, (s + k) % SEQ)

    for k in range(1, SEQ):
        x_copy(k, s).start()

    for ld in loads[1:2]:
        ld.wait()
    ow_send[...] = jnp.zeros((8, HW), F32)
    ow_send[0:COLS, :] = ow_ref[...].astype(F32)

    def w1_copy(k, source):
        slot = w_land.at[pl.ds(pl.multiple_of(source * 8, 8), 8), :]
        return rcopy(ow_send, slot, w1_s.at[k], w1_r.at[k], dpi((z + k) % ZN, xx), s)

    for k in range(1, ZN):
        w1_copy(k, z).start()
    w_land[pl.ds(pl.multiple_of(z * 8, 8), 8), :] = ow_send[...]

    for ld in (loads[0], *loads[2:4]):
        ld.wait()
    for k in range(SEQ):
        win8[k * PATCH : (k + 1) * PATCH, :] = win_ref[...]
        wskip8[k * PATCH : (k + 1) * PATCH, :] = wskip_ref[...]

    loads[4].wait()
    feature = iota((2 * LANES, 2 * LANES), 0) + y * LANES
    lane2 = iota((2 * LANES, 2 * LANES), 1)
    inner = lane2 % LANES
    head = jnp.where(lane2 < LANES, s, mate)
    pick = jnp.where((inner < HD) & (feature == head * HD + inner), 1.0, 0.0).astype(BF)
    for i in range(3):
        part = dot(qkvw[i], pick).astype(BF)
        wsel[:, i * LANES : (i + 1) * LANES] = part[:, :LANES]
        wsel[:, (3 + i) * LANES : (4 + i) * LANES] = part[:, LANES:]
    for ld in loads[5:12]:
        ld.wait()
    for k in range(1, SEQ):
        x_copy(k, (s - k + SEQ) % SEQ).wait_recv()

    def w2_copy(k, source):
        return rcopy(
            wx.at[xx] if source is None else wx.at[xx],
            wx.at[xx if source is None else source],
            w2_s.at[k],
            w2_r.at[k],
            dpi(z, (xx + k) % XN),
            s,
        )

    def wt_rows(zz):
        return wt.at[pl.ds(pl.multiple_of(zz * 160, 32), 160), :]

    def w3_copy(k, source):
        block = wt_rows(source)
        return rcopy(block, block, w3_s.at[k], w3_r.at[k], dp, ((y + k) % YN) * 2 + c)

    def w4_copy(k, core):
        block = wt_rows(((y - k + YN) % YN) * 2 + core)
        return rcopy(block, block, w4_s.at[k], w4_r.at[k], dp, mate)

    def m_copy(i, core):
        rows = pl.multiple_of((2 * i + core) * ROWS, ROWS)
        return rcopy(msend.at[i], qkv.at[pl.ds(rows, ROWS), :], m_s.at[i], m_r.at[i], dp, mate)

    lane = iota((2 * ROWS, LANES), 1)
    seg_lane = (lane >= HD) & (lane < HD + 16)

    def embed_rows(g):
        begin = [pl.multiple_of((4 * g + 2 * e + c) * ROWS, ROWS) for e in range(2)]
        step = iota((2 * ROWS, 64), 0)
        pos = begin[0] + step + jnp.where(step >= ROWS, ROWS, 0)
        source, first, count = plan_ref[0], plan_ref[1], plan_ref[2]
        start = plan_ref[3] * ROWS + plan_ref[4]
        inside = (pos >= start) & (pos < start + count)
        code = jnp.where(inside, (source * 512 + first - start) + pos, 0)
        code = jnp.sum(code.astype(F32), axis=1, keepdims=True).astype(jnp.int32)
        row_of = code % 512
        shard_of = code // 512
        onehot = jnp.where(iota((2 * ROWS, ROWS), 1) == row_of, 1.0, 0.0).astype(BF)
        spread = dot_nt(onehot, xg[...])
        cols = jnp.where(
            iota((2 * ROWS, SEQ * PATCH), 1) // PATCH == shard_of, spread, 0.0
        ).astype(BF)
        half = (dot(cols, win8[...]) + bin_ref[...].reshape(1, D)) * 0.5
        hidden = (half + half * jnp.tanh(half)).astype(BF)
        emb = dot(hidden, wh[...]) + dot(cols, wskip8[...]) + ob_ref[...].reshape(1, D)
        emb = emb.astype(BF)
        emb_own[2 * g] = emb[:ROWS]
        emb_own[2 * g + 1] = emb[ROWS:]
        return begin, emb

    def project_rows(g, begin, emb):
        wide = emb.astype(F32)
        scale = lax.rsqrt(jnp.mean(wide * wide, axis=-1, keepdims=True) + EPS)
        normed = (wide * scale * gain_ref[...].reshape(1, D)).astype(BF)
        proj = dot(normed, wsel[...]).astype(BF)

        marks = []
        for e in range(2):
            seg_row = seg_ref[:, pl.ds(begin[e], ROWS)]
            match = jnp.where(iota((LANES, ROWS), 0) - HD == seg_row, 1.0, 0.0)
            marks.append(jnp.transpose(match))
        marks = jnp.concatenate(marks, axis=0)
        away = jnp.where(seg_lane, (marks - 1.0) * MASKED, 0.0)
        ones = jnp.where(lane == HD, 1.0, 0.0)
        for h in (1, 0):
            q = proj[:, (3 * h) * LANES : (3 * h + 1) * LANES].astype(F32)
            k = proj[:, (3 * h + 1) * LANES : (3 * h + 2) * LANES].astype(F32)
            v = proj[:, (3 * h + 2) * LANES : (3 * h + 3) * LANES].astype(F32)
            q = q * lax.rsqrt(jnp.sum(q * q, axis=-1, keepdims=True) * (1.0 / HD) + EPS)
            k = k * lax.rsqrt(jnp.sum(k * k, axis=-1, keepdims=True) * (1.0 / HD) + EPS)
            parts = [(q + away).astype(BF), (k + marks).astype(BF), (v + ones).astype(BF)]
            for e in range(2):
                for j in range(3):
                    part = parts[j][e * ROWS : (e + 1) * ROWS]
                    lanes = slice(j * LANES, (j + 1) * LANES)
                    if h:
                        msend[2 * g + e, :, lanes] = part
                    else:
                        qkv[pl.ds(begin[e], ROWS), lanes] = part
            if h:
                m_copy(2 * g, c).start()
                m_copy(2 * g + 1, c).start()

    begin, emb = embed_rows(0)
    for k in range(1, ZN):
        w1_copy(k, (z - k + ZN) % ZN).wait_recv()
    for m in range(5):
        tiles[m] = w_land[:, m * LANES : (m + 1) * LANES]
    block = jnp.concatenate(
        [
            jnp.concatenate([tiles[m, pl.ds(j, ZN, stride=8), :] for j in range(COLS)], axis=0)
            for m in range(5)
        ],
        axis=1,
    )
    block = jnp.concatenate([block, jnp.zeros((8, HW), F32)], axis=0)
    wx[xx] = block.astype(BF)
    for k in range(1, XN):
        w2_copy(k, None).start()
    project_rows(0, begin, emb)
    for k in range(1, XN):
        w2_copy(k, (xx - k + XN) % XN).wait_recv()
    block = jnp.concatenate([wx[j, 0:GROUP, :].astype(F32) for j in range(XN)], axis=0)
    wt[pl.ds(pl.multiple_of(s * 160, 32), 160), :] = block.astype(BF)
    for k in range(1, YN):
        w3_copy(k, s).start()
    w4_copy(0, c).start()
    project_rows(1, *embed_rows(1))
    factor = hs_ref[s] * (LOG2E / math.sqrt(HD))
    causal = iota((ROWS, ROWS), 0) >= iota((ROWS, ROWS), 1)

    def head_rows(core, head):
        return ret.at[core, pl.ds(pl.multiple_of(head * HD, 16), HD), :]

    def a_copy(block, source, k, core):
        rows = head_rows(core, source)
        return rcopy(att_send.at[block], rows, a_s.at[k], a_r.at[k], dp, (s + k) % SEQ)

    def c_copy():
        return rcopy(cot_t.at[1 - c], cot_m, c_s.at[0], c_r.at[0], dp, mate)

    def cotangent_columns():
        loads[12].wait()
        for m in range(3):
            cot_f[m] = jnp.transpose(cot[m * LANES : (m + 1) * LANES, :].astype(F32))
        for core in range(2):
            for j in range(YN):
                base = [x2 * GROUP + (2 * j + core) * COLS + n for x2 in range(XN) for n in range(COLS)]
                for m in range(3):
                    rows = [cot_f[m, pl.ds(first, ZN, stride=160), :] for first in base]
                    rows = jnp.concatenate(rows, axis=0).astype(BF)
                    cot_t[core, j * 160 : (j + 1) * 160, m * LANES : (m + 1) * LANES] = rows
        c_copy().start()

    for i in range(2):
        m_copy(i, 1 - c).wait_recv()
    for b in (3, 2, 7, 0, 5, 1, 6, 4):
        if b == 7:
            for i in range(2, 4):
                m_copy(i, 1 - c).wait_recv()
        q = qkv[b * ROWS : (b + 1) * ROWS, 0:LANES]
        total = jnp.zeros((ROWS, LANES), F32)
        edges = list(range(0, b * ROWS, 2 * ROWS)) + [b * ROWS]
        for lo, hi in zip(edges[:-1], edges[1:]):
            scores = dot_nt(q, qkv[lo:hi, LANES : 2 * LANES]) * factor
            total = total + dot(jnp.exp2(scores).astype(BF), qkv[lo:hi, 2 * LANES : 3 * LANES])
        lo, hi = b * ROWS, (b + 1) * ROWS
        scores = dot_nt(q, qkv[lo:hi, LANES : 2 * LANES]) * factor
        weights = jnp.where(causal, jnp.exp2(scores), 0.0).astype(BF)
        total = total + dot(weights, qkv[lo:hi, 2 * LANES : 3 * LANES])
        across = jnp.transpose(total)
        out = (across[0:HD, :] / across[HD : HD + 1, :]).astype(BF)
        att_send[b] = out

        @pl.when(s == b)
        def _():
            ret[c, pl.ds(pl.multiple_of(s * HD, 16), HD), :] = out

        @pl.when(s != b)
        def _():
            a_copy(b, s, (b - s + SEQ) % SEQ, b % 2).start()

        if b == 0:
            cotangent_columns()
        if b == 5:
            for k in range(1, YN):
                w3_copy(k, ((y - k + YN) % YN) * 2 + c).wait_recv()
                w4_copy(k, c).start()

    for k in range(YN):
        w4_copy(k, 1 - c).wait_recv()
    for t in range(SEQ):
        block = wt[t * 160 : (t + 1) * 160, :].astype(F32)
        for x2 in range(XN):
            for n in range(COLS):
                first = x2 * GROUP + n * ZN
                rows = pl.ds(x2 * GROUP + t * COLS + n, ZN, stride=160)
                for m in range(5):
                    wt_f[m, rows, :] = block[first : first + ZN, m * LANES : (m + 1) * LANES]

    def pass_on(head, core):
        return rcopy(
            head_rows(core, head), head_rows(core, head), p_s.at[head], p_r.at[head], dp, mate
        )

    pass_on(s, c).start()
    for k in range(1, SEQ):
        head = (s - k + SEQ) % SEQ
        a_copy(0, head, k, c).wait_recv()
        pass_on(head, c).start()

    attended = ret[c]
    order = [2, 1, 3, 0]

    def owner_rows(k):
        return pl.ds(pl.multiple_of(((y + k) % YN) * 160, 32), 160)

    p_own[...] = dot_nt(cot_t[c], attended)
    c_copy().wait_recv()
    for head in range(SEQ):
        pass_on(head, 1 - c).wait_recv()
    other = ret[1 - c]

    def ya_copy(k):
        to = (y + k) % YN
        return rcopy(ya.at[to], ya_land.at[k], ya_s.at[k], ya_r.at[k], dp, to * 2 + c)

    def xb_copy(k, row):
        to = (xx + k) % XN
        slot = k * YN + row
        return rcopy(
            xb.at[to, row], xb_land.at[k, row], xb_s.at[slot], xb_r.at[slot], dpi(z, to), s
        )

    pad = jnp.zeros((8, HW - ROWS), F32)
    for k in order:
        to = (y + k) % YN
        piece = p_own[owner_rows(k), :] + dot_nt(cot_m[owner_rows(k), :], other)
        p_own[owner_rows(k), :] = piece
        if k:
            ya[to] = piece[:, 0:ROWS].astype(BF)
            ya_copy(k).start()
        for j in range(XN):
            part = piece[j * GROUP : (j + 1) * GROUP, ROWS:]
            xb[j, to] = jnp.concatenate([part, pad], axis=0).astype(BF)
        for j in (2, 1, 3):
            xb_copy(j, to).start()

    rows = jnp.transpose(attended)
    for j in range(5):
        cols = slice(j * 256, (j + 1) * 256)
        weight = jnp.concatenate([wt_f[m, cols, :].astype(BF) for m in range(5)], axis=1)
        branch = dot_nt(rows, weight)
        lo_ref[:, cols] = (emb_own[y, :, cols].astype(F32) + branch).astype(BF)

    for k in range(1, YN):
        ya_copy(k).wait_recv()
    own = p_own[pl.ds(pl.multiple_of(y * 160, 32), 160), :]
    a_sum = own[:, 0:ROWS]
    for k in range(1, YN):
        a_sum = a_sum + ya_land[k].astype(F32)
    pad = jnp.zeros((8, ROWS), F32)
    block40[...] = jnp.zeros_like(block40)
    for j in range(XN):
        piece = a_sum[j * GROUP : (j + 1) * GROUP, :]
        ax[j] = jnp.concatenate([piece, pad], axis=0).astype(BF)

        @pl.when(xx == j)
        def _():
            block40[:, 0:ROWS] = piece

    def ax_copy(k):
        to = (xx + k) % XN
        return rcopy(ax.at[to], ax_land.at[k], ax_s.at[k], ax_r.at[k], dpi(z, to), s)

    for k in range(1, XN):
        ax_copy(k).start()

    for k in range(1, XN):
        for j in range(YN):
            xb_copy(k, j).wait_recv()
    pad = jnp.zeros((8, HW - ROWS), F32)
    for j in range(YN):
        begin = pl.multiple_of((j * XN + xx) * GROUP, 8)
        piece = p_own[pl.ds(begin, GROUP), ROWS:HW]
        for k in range(1, XN):
            piece = piece + xb_land[k, j].astype(F32)[0:GROUP, :]
        by[j] = jnp.concatenate([piece, pad], axis=0).astype(BF)

        @pl.when(y == j)
        def _():
            block40[:, ROWS:HW] = piece

    def by_copy(k):
        to = (y + k) % YN
        return rcopy(by.at[to], by_land.at[k], by_s.at[k], by_r.at[k], dp, to * 2 + c)

    for k in range(1, YN):
        by_copy(k).start()
    for k in range(1, XN):
        ax_copy(k).wait_recv()
    for k in range(1, YN):
        by_copy(k).wait_recv()
    left = block40[:, 0:ROWS]
    right = block40[:, ROWS:HW]
    for k in range(1, XN):
        left = left + ax_land[k].astype(F32)[0:GROUP, :]
        right = right + by_land[k].astype(F32)[0:GROUP, :]
    block40[:, 0:ROWS] = left
    block40[:, ROWS:HW] = right
    for m in range(5):
        tiles[m, 0:GROUP, :] = block40[:, m * LANES : (m + 1) * LANES]
    for j in range(ZN):
        for m in range(5):
            part = tiles[m, pl.ds(j, COLS, stride=ZN), :]
            fs_f[j, m * COLS : (m + 1) * COLS, :] = part
    fs[...] = fs_f[...].astype(BF)

    def f_copy(k):
        to = (z + k) % ZN
        return rcopy(fs.at[to], fs_land.at[k], f_s.at[k], f_r.at[k], dpi(to, xx), s)

    for k in (4, 3, 5, 2, 6, 1, 7):
        f_copy(k).start()
    final = fs_f[z]
    for k in range(1, ZN):
        f_copy(k).wait_recv()
        final = final + fs_land[k].astype(F32)
    fs_f[0] = final
    for m in range(COLS):
        og_ref[:, m * LANES : (m + 1) * LANES] = fs_f[0, m * COLS : (m + 1) * COLS, :]

    for k in range(1, SEQ):
        x_copy(k, s).wait_send()
        a_copy(0, s, k, (s + k) % 2).wait_send()
    for k in range(1, ZN):
        w1_copy(k, z).wait_send()
        f_copy(k).wait_send()
    for k in range(1, XN):
        w2_copy(k, None).wait_send()
        w3_copy(k, s).wait_send()
        ya_copy(k).wait_send()
        for j in range(YN):
            xb_copy(k, j).wait_send()
        ax_copy(k).wait_send()
        by_copy(k).wait_send()
    for k in range(YN):
        w4_copy(k, c).wait_send()
        m_copy(k, c).wait_send()
    for head in range(SEQ):
        pass_on(head, c).wait_send()
    c_copy().wait_send()


def hand_over(lo_in, og_in, lo_out, og_out, lo_vmem, og_vmem, sem_in, sem_out):
    def parts(lo, og):
        rows = [pl.ds(k * 128, 128) for k in range(3)]
        return [lo.at[r, :] for r in rows] + [og]

    held = parts(lo_vmem, og_vmem)
    into = [
        pltpu.make_async_copy(a, b, sem_in.at[k])
        for k, (a, b) in enumerate(zip(parts(lo_in, og_in), held))
    ]
    back = [
        pltpu.make_async_copy(a, b, sem_out.at[k])
        for k, (a, b) in enumerate(zip(held, parts(lo_out, og_out)))
    ]
    for copy in into:
        copy.start()
    for a, b in zip(into, back):
        a.wait()
        b.start()
    for copy in back:
        copy.wait()


def per_device(
    patches,
    segment_ids,
    regroup_plan,
    input_weight,
    input_bias,
    skip_weight,
    hidden_weight,
    output_bias,
    norm_gain,
    head_scale,
    qkv_weight,
    out_weight,
    cotangent,
):
    vmem = pl.BlockSpec(memory_space=pltpu.VMEM)
    hbm = pl.BlockSpec(memory_space=pltpu.HBM)
    dma = pltpu.SemaphoreType.DMA
    scratch = [
        pltpu.VMEM((1, WIN), jnp.int32),
        pltpu.VMEM((5, 1, 64), jnp.int32),
        pltpu.VMEM((PATCH, D), BF),
        pltpu.VMEM((D,), F32),
        pltpu.VMEM((PATCH, D), BF),
        pltpu.VMEM((D,), F32),
        pltpu.VMEM((D,), F32),
        pltpu.SMEM((SEQ,), F32),
        pltpu.VMEM((COLS, HW), BF),
        pltpu.VMEM((D, D), BF),
        pltpu.VMEM((3, D, 2 * LANES), BF),
        pltpu.VMEM((ROWS, D), BF),
        pltpu.VMEM((3, D, LANES), F32),
        pltpu.VMEM((2, HW, ROWS), BF),
        pltpu.VMEM((SEQ * PATCH, ROWS), BF),
        pltpu.VMEM((SEQ * PATCH, D), BF),
        pltpu.VMEM((SEQ * PATCH, D), BF),
        pltpu.VMEM((D, 6 * LANES), BF),
        pltpu.VMEM((WIN, 3 * LANES), BF),
        pltpu.VMEM((4, ROWS, 3 * LANES), BF),
        pltpu.VMEM((4, ROWS, D), BF),
        pltpu.VMEM((8, HW), F32),
        pltpu.VMEM((ZN * 8, HW), F32),
        pltpu.VMEM((XN, 48, HW), BF),
        pltpu.VMEM((D, HW), BF),
        pltpu.VMEM((5, D, LANES), F32),
        pltpu.VMEM((5, 64, LANES), F32),
        pltpu.VMEM((SEQ, HD, ROWS), BF),
        pltpu.VMEM((2, HW, ROWS), BF),
        pltpu.VMEM((HW, HW), F32),
        pltpu.VMEM((HW, ROWS), BF),
        pltpu.VMEM((YN, 160, ROWS), BF),
        pltpu.VMEM((YN, 160, ROWS), BF),
        pltpu.VMEM((XN, YN, 48, HW - ROWS), BF),
        pltpu.VMEM((XN, YN, 48, HW - ROWS), BF),
        pltpu.VMEM((XN, 48, ROWS), BF),
        pltpu.VMEM((XN, 48, ROWS), BF),
        pltpu.VMEM((YN, 48, HW - ROWS), BF),
        pltpu.VMEM((YN, 48, HW - ROWS), BF),
        pltpu.VMEM((GROUP, HW), F32),
        pltpu.VMEM((ZN, 32, LANES), F32),
        pltpu.VMEM((ZN, 32, LANES), BF),
        pltpu.VMEM((ZN, 32, LANES), BF),
        dma((13,)),
        dma((8,)),
        dma((8,)),
        dma((8,)),
        dma((8,)),
        dma((4,)),
        dma((4,)),
        dma((4,)),
        dma((4,)),
        dma((4,)),
        dma((4,)),
        dma((4,)),
        dma((4,)),
        dma((8,)),
        dma((8,)),
        dma((8,)),
        dma((8,)),
        dma((1,)),
        dma((1,)),
        dma((4,)),
        dma((4,)),
        dma((16,)),
        dma((16,)),
        dma((4,)),
        dma((4,)),
        dma((4,)),
        dma((4,)),
        dma((8,)),
        dma((8,)),
    ]
    layer_out, grad = pl.pallas_call(
        whole_layer,
        out_shape=(
            jax.ShapeDtypeStruct((ROWS, D), BF),
            jax.ShapeDtypeStruct((COLS, HW), F32),
        ),
        in_specs=[hbm] * 13,
        out_specs=(vmem, vmem),
        scratch_shapes=scratch,
        compiler_params=pltpu.CompilerParams(
            collective_id=0, has_side_effects=True, vmem_limit_bytes=63 * 1024 * 1024
        ),
        name="whole_layer",
    )(
        patches,
        segment_ids,
        jnp.transpose(regroup_plan, (1, 0, 2)),
        input_weight,
        input_bias,
        skip_weight,
        hidden_weight,
        output_bias,
        norm_gain,
        head_scale,
        jnp.transpose(qkv_weight, (1, 0, 2)),
        jnp.transpose(out_weight),
        cotangent,
    )
    layer_out, grad = pl.pallas_call(
        hand_over,
        out_shape=(
            jax.ShapeDtypeStruct((ROWS, D), BF),
            jax.ShapeDtypeStruct((COLS, HW), F32),
        ),
        in_specs=[hbm, hbm],
        out_specs=(hbm, hbm),
        scratch_shapes=[
            pltpu.VMEM((ROWS, D), BF),
            pltpu.VMEM((COLS, HW), F32),
            dma((4,)),
            dma((4,)),
        ],
        name="hand_over",
    )(layer_out, grad)
    return layer_out, jnp.transpose(grad)


def solution(mesh):
    placed = (
        P(None, ("dp", "seq")),
        P("dp", None),
        P("dp", None, None),
        P(),
        P(),
        P(),
        P(),
        P(),
        P(),
        P(),
        P(),
        P(None, ("dp", "seq")),
        P(("dp", "seq"), None),
    )
    return jax.shard_map(
        per_device,
        mesh=mesh,
        in_specs=placed,
        out_specs=(P(("dp", "seq"), None), P(None, ("dp", "seq"))),
        check_vma=False,
    )
```

```python
import functools
import math

import jax
import jax.numpy as jnp
from jax import lax
from jax.experimental import pallas as pl
from jax.experimental.pallas import tpu as pltpu
from jax.sharding import PartitionSpec as P

HD = 80
LANES = 128
ZN, XN, YN = 8, 4, 4
SEQ = 8
ROWS = 384
WIN = ROWS * SEQ
D = 1280
HW = 640
PATCH = 32
COLS = 5
GROUP = COLS * SEQ
EPS = 1e-06
MASKED = 2048.0
LOG2E = 1.4426950408889634
MESH = pl.DeviceIdType.MESH
BF = jnp.bfloat16
F32 = jnp.float32
NT = (((1,), (1,)), ((), ()))


def iota(shape, dim):
    return lax.broadcasted_iota(jnp.int32, shape, dim)


def dot(a, b):
    return jnp.dot(a, b, preferred_element_type=F32)


def dot_nt(a, b):
    return lax.dot_general(a, b, NT, preferred_element_type=F32)


def whole_layer(
    x_hbm,
    seg_hbm,
    plan_hbm,
    win_hbm,
    bin_hbm,
    wskip_hbm,
    wh_hbm,
    ob_hbm,
    gain_hbm,
    hs_hbm,
    qkvw_hbm,
    ow_hbm,
    cot_hbm,
    lo_ref,
    og_ref,
    seg_ref,
    plan_ref,
    win_ref,
    bin_ref,
    wskip_ref,
    ob_ref,
    gain_ref,
    hs_ref,
    ow_ref,
    wh,
    qkvw,
    cot,
    cot_f,
    cot_t,
    xg,
    win8,
    wsel,
    qkv,
    msend,
    emb_own,
    ow_send,
    w_land,
    wx,
    wt,
    wt_f,
    tiles,
    att_send,
    ret,
    p_own,
    cot_m,
    ya,
    ya_land,
    xb,
    xb_land,
    ax,
    ax_land,
    by,
    by_land,
    block40,
    fs_f,
    fs,
    fs_land,
    ld_sem,
    x_s,
    x_r,
    w1_s,
    w1_r,
    w2_s,
    w2_r,
    w3_s,
    w3_r,
    w4_s,
    w4_r,
    m_s,
    m_r,
    a_s,
    a_r,
    p_s,
    p_r,
    c_s,
    c_r,
    ya_s,
    ya_r,
    xb_s,
    xb_r,
    ax_s,
    ax_r,
    by_s,
    by_r,
    f_s,
    f_r,
):
    dp = lax.axis_index("dp")
    s = lax.axis_index("seq")
    z = dp // XN
    xx = dp % XN
    y = s // 2
    c = s % 2
    mate = y * 2 + (1 - c)
    def rcopy(src, dst, ssem, rsem, dp_t, seq_t):
        return pltpu.make_async_remote_copy(
            src_ref=src,
            dst_ref=dst,
            send_sem=ssem,
            recv_sem=rsem,
            device_id=(dp_t, seq_t),
            device_id_type=MESH,
        )

    def dpi(zz, x2):
        return zz * XN + x2

    bar = pltpu.get_barrier_semaphore()

    def greet(dp_t, seq_t):
        pl.semaphore_signal(bar, inc=1, device_id=(dp_t, seq_t), device_id_type=MESH)

    for k in range(1, SEQ):
        greet(dp, (s + k) % SEQ)
    for k in range(1, XN):
        greet(dpi(z, (xx + k) % XN), s)
    for k in range(1, ZN):
        greet(dpi((z + k) % ZN, xx), s)

    loads = [
        pltpu.make_async_copy(src, dst, ld_sem.at[i])
        for i, (src, dst) in enumerate(
            [
                (x_hbm, xg.at[pl.ds(pl.multiple_of(s * PATCH, PATCH), PATCH), :]),
                (ow_hbm, ow_ref),
                (win_hbm, win_ref),
                (wskip_hbm, wskip_ref),
                (qkvw_hbm.at[:, :, pl.ds(pl.multiple_of(y * LANES, LANES), 2 * LANES)], qkvw),
                (plan_hbm, plan_ref),
                (seg_hbm, seg_ref),
                (bin_hbm, bin_ref),
                (ob_hbm, ob_ref),
                (gain_hbm, gain_ref),
                (hs_hbm, hs_ref),
                (wh_hbm, wh.at[pl.ds(0, D), :]),
                (cot_hbm, cot),
            ]
        )
    ]
    for ld in loads:
        ld.start()

    pl.semaphore_wait(bar, 7 + 3 + 7)

    def x_copy(k, source):
        rows = xg.at[pl.ds(pl.multiple_of(source * PATCH, PATCH), PATCH), :]
        return rcopy(x_hbm, rows, x_s.at[k], x_r.at[k], dp, (s + k) % SEQ)

    for k in range(1, SEQ):
        x_copy(k, s).start()

    for ld in loads[1:2]:
        ld.wait()
    ow_send[...] = jnp.zeros((8, HW), F32)
    ow_send[0:COLS, :] = ow_ref[...].astype(F32)

    def w1_copy(k, source):
        slot = w_land.at[pl.ds(pl.multiple_of(source * 8, 8), 8), :]
        return rcopy(ow_send, slot, w1_s.at[k], w1_r.at[k], dpi((z + k) % ZN, xx), s)

    for k in range(1, ZN):
        w1_copy(k, z).start()
    w_land[pl.ds(pl.multiple_of(z * 8, 8), 8), :] = ow_send[...]

    for ld in (loads[0], *loads[2:4]):
        ld.wait()
    for k in range(SEQ):
        win8[k * PATCH : (k + 1) * PATCH, :] = win_ref[...]
        wh[D + k * PATCH : D + (k + 1) * PATCH, :] = wskip_ref[...]

    loads[4].wait()
    feature = iota((2 * LANES, 2 * LANES), 0) + y * LANES
    lane2 = iota((2 * LANES, 2 * LANES), 1)
    inner = lane2 % LANES
    head = jnp.where(lane2 < LANES, s, mate)
    pick = jnp.where((inner < HD) & (feature == head * HD + inner), 1.0, 0.0).astype(BF)
    for i in range(3):
        part = dot(qkvw[i], pick).astype(BF)
        wsel[:, i * LANES : (i + 1) * LANES] = part[:, :LANES]
        wsel[:, (3 + i) * LANES : (4 + i) * LANES] = part[:, LANES:]
    for ld in loads[5:12]:
        ld.wait()
    for k in range(1, SEQ):
        x_copy(k, (s - k + SEQ) % SEQ).wait_recv()

    def w2_copy(k, source):
        return rcopy(
            wx.at[xx] if source is None else wx.at[xx],
            wx.at[xx if source is None else source],
            w2_s.at[k],
            w2_r.at[k],
            dpi(z, (xx + k) % XN),
            s,
        )

    def wt_rows(zz):
        return wt.at[pl.ds(pl.multiple_of(zz * 160, 32), 160), :]

    def w3_copy(k, source):
        block = wt_rows(source)
        return rcopy(block, block, w3_s.at[k], w3_r.at[k], dp, ((y + k) % YN) * 2 + c)

    def w4_copy(k, core):
        block = wt_rows(((y - k + YN) % YN) * 2 + core)
        return rcopy(block, block, w4_s.at[k], w4_r.at[k], dp, mate)

    def m_copy(i, core):
        rows = pl.multiple_of((2 * i + core) * ROWS, ROWS)
        return rcopy(msend.at[i], qkv.at[pl.ds(rows, ROWS), :], m_s.at[i], m_r.at[i], dp, mate)

    lane = iota((2 * ROWS, LANES), 1)
    seg_lane = (lane >= HD) & (lane < HD + 16)

    def embed_rows(g):
        begin = [pl.multiple_of((4 * g + 2 * e + c) * ROWS, ROWS) for e in range(2)]
        step = iota((2 * ROWS, 64), 0)
        pos = begin[0] + step + jnp.where(step >= ROWS, ROWS, 0)
        source, first, count = plan_ref[0], plan_ref[1], plan_ref[2]
        start = plan_ref[3] * ROWS + plan_ref[4]
        inside = (pos >= start) & (pos < start + count)
        code = jnp.where(inside, (source * 512 + first - start) + pos, 0)
        code = jnp.sum(code.astype(F32), axis=1, keepdims=True).astype(jnp.int32)
        row_of = code % 512
        shard_of = code // 512
        onehot = jnp.where(iota((2 * ROWS, ROWS), 1) == row_of, 1.0, 0.0).astype(BF)
        spread = dot_nt(onehot, xg[...])
        cols = jnp.where(
            iota((2 * ROWS, SEQ * PATCH), 1) // PATCH == shard_of, spread, 0.0
        ).astype(BF)
        half = (dot(cols, win8[...]) + bin_ref[...].reshape(1, D)) * 0.5
        hidden = (half + half * jnp.tanh(half)).astype(BF)
        both = jnp.concatenate([hidden, cols], axis=1)
        emb = (dot(both, wh[...]) + ob_ref[...].reshape(1, D)).astype(BF)
        emb_own[2 * g] = emb[:ROWS]
        emb_own[2 * g + 1] = emb[ROWS:]
        return begin, emb

    def project_rows(g, begin, emb):
        wide = emb.astype(F32)
        scale = lax.rsqrt(jnp.mean(wide * wide, axis=-1, keepdims=True) + EPS)
        normed = (wide * scale * gain_ref[...].reshape(1, D)).astype(BF)
        proj = dot(normed, wsel[...]).astype(BF)

        marks = []
        for e in range(2):
            seg_row = seg_ref[:, pl.ds(begin[e], ROWS)]
            match = jnp.where(iota((LANES, ROWS), 0) - HD == seg_row, 1.0, 0.0)
            marks.append(jnp.transpose(match))
        marks = jnp.concatenate(marks, axis=0)
        away = jnp.where(seg_lane, (marks - 1.0) * MASKED, 0.0)
        ones = jnp.where(lane == HD, 1.0, 0.0)
        for h in (1, 0):
            q = proj[:, (3 * h) * LANES : (3 * h + 1) * LANES].astype(F32)
            k = proj[:, (3 * h + 1) * LANES : (3 * h + 2) * LANES].astype(F32)
            v = proj[:, (3 * h + 2) * LANES : (3 * h + 3) * LANES].astype(F32)
            q = q * lax.rsqrt(jnp.sum(q * q, axis=-1, keepdims=True) * (1.0 / HD) + EPS)
            k = k * lax.rsqrt(jnp.sum(k * k, axis=-1, keepdims=True) * (1.0 / HD) + EPS)
            parts = [(q + away).astype(BF), (k + marks).astype(BF), (v + ones).astype(BF)]
            for e in range(2):
                for j in range(3):
                    part = parts[j][e * ROWS : (e + 1) * ROWS]
                    lanes = slice(j * LANES, (j + 1) * LANES)
                    if h:
                        msend[2 * g + e, :, lanes] = part
                    else:
                        qkv[pl.ds(begin[e], ROWS), lanes] = part
            if h:
                m_copy(2 * g, c).start()
                m_copy(2 * g + 1, c).start()

    begin, emb = embed_rows(0)
    for k in range(1, ZN):
        w1_copy(k, (z - k + ZN) % ZN).wait_recv()
    for m in range(5):
        tiles[m] = w_land[:, m * LANES : (m + 1) * LANES]
    block = jnp.concatenate(
        [
            jnp.concatenate([tiles[m, pl.ds(j, ZN, stride=8), :] for j in range(COLS)], axis=0)
            for m in range(5)
        ],
        axis=1,
    )
    block = jnp.concatenate([block, jnp.zeros((8, HW), F32)], axis=0)
    wx[xx] = block.astype(BF)
    for k in range(1, XN):
        w2_copy(k, None).start()
    project_rows(0, begin, emb)
    for k in range(1, XN):
        w2_copy(k, (xx - k + XN) % XN).wait_recv()
    block = jnp.concatenate([wx[j, 0:GROUP, :].astype(F32) for j in range(XN)], axis=0)
    wt[pl.ds(pl.multiple_of(s * 160, 32), 160), :] = block.astype(BF)
    for k in range(1, YN):
        w3_copy(k, s).start()
    w4_copy(0, c).start()
    project_rows(1, *embed_rows(1))
    factor = hs_ref[s] * (LOG2E / math.sqrt(HD))
    causal = iota((ROWS, ROWS), 0) >= iota((ROWS, ROWS), 1)

    def head_rows(core, head):
        return ret.at[core, pl.ds(pl.multiple_of(head * HD, 16), HD), :]

    def a_copy(block, source, k, core):
        rows = head_rows(core, source)
        return rcopy(att_send.at[block], rows, a_s.at[k], a_r.at[k], dp, (s + k) % SEQ)

    def c_copy():
        return rcopy(cot_t.at[1 - c], cot_m, c_s.at[0], c_r.at[0], dp, mate)

    def cotangent_columns():
        loads[12].wait()
        for m in range(3):
            cot_f[m] = jnp.transpose(cot[m * LANES : (m + 1) * LANES, :].astype(F32))
        for core in range(2):
            for j in range(YN):
                base = [x2 * GROUP + (2 * j + core) * COLS + n for x2 in range(XN) for n in range(COLS)]
                for m in range(3):
                    rows = [cot_f[m, pl.ds(first, ZN, stride=160), :] for first in base]
                    rows = jnp.concatenate(rows, axis=0).astype(BF)
                    cot_t[core, j * 160 : (j + 1) * 160, m * LANES : (m + 1) * LANES] = rows
        c_copy().start()

    for i in range(2):
        m_copy(i, 1 - c).wait_recv()
    for b in (3, 2, 7, 0, 5, 1, 6, 4):
        if b == 7:
            for i in range(2, 4):
                m_copy(i, 1 - c).wait_recv()
        q = qkv[b * ROWS : (b + 1) * ROWS, 0:LANES]
        total = jnp.zeros((ROWS, LANES), F32)
        edges = list(range(0, b * ROWS, 2 * ROWS)) + [b * ROWS]
        for lo, hi in zip(edges[:-1], edges[1:]):
            scores = dot_nt(q, qkv[lo:hi, LANES : 2 * LANES]) * factor
            total = total + dot(jnp.exp2(scores).astype(BF), qkv[lo:hi, 2 * LANES : 3 * LANES])
        lo, hi = b * ROWS, (b + 1) * ROWS
        scores = dot_nt(q, qkv[lo:hi, LANES : 2 * LANES]) * factor
        weights = jnp.where(causal, jnp.exp2(scores), 0.0).astype(BF)
        total = total + dot(weights, qkv[lo:hi, 2 * LANES : 3 * LANES])
        across = jnp.transpose(total)
        out = (across[0:HD, :] / across[HD : HD + 1, :]).astype(BF)
        att_send[b] = out

        @pl.when(s == b)
        def _():
            ret[c, pl.ds(pl.multiple_of(s * HD, 16), HD), :] = out

        @pl.when(s != b)
        def _():
            a_copy(b, s, (b - s + SEQ) % SEQ, b % 2).start()

        if b == 0:
            cotangent_columns()
        if b == 5:
            for k in range(1, YN):
                w3_copy(k, ((y - k + YN) % YN) * 2 + c).wait_recv()
                w4_copy(k, c).start()

    for k in range(YN):
        w4_copy(k, 1 - c).wait_recv()
    for t in range(SEQ):
        block = wt[t * 160 : (t + 1) * 160, :].astype(F32)
        for x2 in range(XN):
            for n in range(COLS):
                first = x2 * GROUP + n * ZN
                rows = pl.ds(x2 * GROUP + t * COLS + n, ZN, stride=160)
                for m in range(5):
                    wt_f[m, rows, :] = block[first : first + ZN, m * LANES : (m + 1) * LANES]

    def pass_on(head, core):
        return rcopy(
            head_rows(core, head), head_rows(core, head), p_s.at[head], p_r.at[head], dp, mate
        )

    pass_on(s, c).start()
    for k in range(1, SEQ):
        head = (s - k + SEQ) % SEQ
        a_copy(0, head, k, c).wait_recv()
        pass_on(head, c).start()

    attended = ret[c]
    order = [2, 1, 3, 0]

    def owner_rows(k):
        return pl.ds(pl.multiple_of(((y + k) % YN) * 160, 32), 160)

    p_own[...] = dot_nt(cot_t[c], attended)
    c_copy().wait_recv()
    for head in range(SEQ):
        pass_on(head, 1 - c).wait_recv()
    other = ret[1 - c]

    def ya_copy(k):
        to = (y + k) % YN
        return rcopy(ya.at[to], ya_land.at[k], ya_s.at[k], ya_r.at[k], dp, to * 2 + c)

    def xb_copy(k, row):
        to = (xx + k) % XN
        slot = k * YN + row
        return rcopy(
            xb.at[to, row], xb_land.at[k, row], xb_s.at[slot], xb_r.at[slot], dpi(z, to), s
        )

    pad = jnp.zeros((8, HW - ROWS), F32)
    for k in order:
        to = (y + k) % YN
        piece = p_own[owner_rows(k), :] + dot_nt(cot_m[owner_rows(k), :], other)
        p_own[owner_rows(k), :] = piece
        if k:
            ya[to] = piece[:, 0:ROWS].astype(BF)
            ya_copy(k).start()
        for j in range(XN):
            part = piece[j * GROUP : (j + 1) * GROUP, ROWS:]
            xb[j, to] = jnp.concatenate([part, pad], axis=0).astype(BF)
        for j in (2, 1, 3):
            xb_copy(j, to).start()

    rows = jnp.transpose(attended)
    for j in range(5):
        cols = slice(j * 256, (j + 1) * 256)
        weight = jnp.concatenate([wt_f[m, cols, :].astype(BF) for m in range(5)], axis=1)
        branch = dot_nt(rows, weight)
        lo_ref[:, cols] = (emb_own[y, :, cols].astype(F32) + branch).astype(BF)

    for k in range(1, YN):
        ya_copy(k).wait_recv()
    own = p_own[pl.ds(pl.multiple_of(y * 160, 32), 160), :]
    a_sum = own[:, 0:ROWS]
    for k in range(1, YN):
        a_sum = a_sum + ya_land[k].astype(F32)
    pad = jnp.zeros((8, ROWS), F32)
    block40[...] = jnp.zeros_like(block40)
    for j in range(XN):
        piece = a_sum[j * GROUP : (j + 1) * GROUP, :]
        ax[j] = jnp.concatenate([piece, pad], axis=0).astype(BF)

        @pl.when(xx == j)
        def _():
            block40[:, 0:ROWS] = piece

    def ax_copy(k):
        to = (xx + k) % XN
        return rcopy(ax.at[to], ax_land.at[k], ax_s.at[k], ax_r.at[k], dpi(z, to), s)

    for k in range(1, XN):
        ax_copy(k).start()

    for k in range(1, XN):
        for j in range(YN):
            xb_copy(k, j).wait_recv()
    pad = jnp.zeros((8, HW - ROWS), F32)
    for j in range(YN):
        begin = pl.multiple_of((j * XN + xx) * GROUP, 8)
        piece = p_own[pl.ds(begin, GROUP), ROWS:HW]
        for k in range(1, XN):
            piece = piece + xb_land[k, j].astype(F32)[0:GROUP, :]
        by[j] = jnp.concatenate([piece, pad], axis=0).astype(BF)

        @pl.when(y == j)
        def _():
            block40[:, ROWS:HW] = piece

    def by_copy(k):
        to = (y + k) % YN
        return rcopy(by.at[to], by_land.at[k], by_s.at[k], by_r.at[k], dp, to * 2 + c)

    for k in range(1, YN):
        by_copy(k).start()
    for k in range(1, XN):
        ax_copy(k).wait_recv()
    for k in range(1, YN):
        by_copy(k).wait_recv()
    left = block40[:, 0:ROWS]
    right = block40[:, ROWS:HW]
    for k in range(1, XN):
        left = left + ax_land[k].astype(F32)[0:GROUP, :]
        right = right + by_land[k].astype(F32)[0:GROUP, :]
    block40[:, 0:ROWS] = left
    block40[:, ROWS:HW] = right
    for m in range(5):
        tiles[m, 0:GROUP, :] = block40[:, m * LANES : (m + 1) * LANES]
    for j in range(ZN):
        for m in range(5):
            part = tiles[m, pl.ds(j, COLS, stride=ZN), :]
            fs_f[j, m * COLS : (m + 1) * COLS, :] = part
    fs[...] = fs_f[...].astype(BF)

    def f_copy(k):
        to = (z + k) % ZN
        return rcopy(fs.at[to], fs_land.at[k], f_s.at[k], f_r.at[k], dpi(to, xx), s)

    for k in (4, 3, 5, 2, 6, 1, 7):
        f_copy(k).start()
    final = fs_f[z]
    for k in range(1, ZN):
        f_copy(k).wait_recv()
        final = final + fs_land[k].astype(F32)
    fs_f[0] = final
    for m in range(COLS):
        og_ref[:, m * LANES : (m + 1) * LANES] = fs_f[0, m * COLS : (m + 1) * COLS, :]

    for k in range(1, SEQ):
        x_copy(k, s).wait_send()
        a_copy(0, s, k, (s + k) % 2).wait_send()
    for k in range(1, ZN):
        w1_copy(k, z).wait_send()
        f_copy(k).wait_send()
    for k in range(1, XN):
        w2_copy(k, None).wait_send()
        w3_copy(k, s).wait_send()
        ya_copy(k).wait_send()
        for j in range(YN):
            xb_copy(k, j).wait_send()
        ax_copy(k).wait_send()
        by_copy(k).wait_send()
    for k in range(YN):
        w4_copy(k, c).wait_send()
        m_copy(k, c).wait_send()
    for head in range(SEQ):
        pass_on(head, c).wait_send()
    c_copy().wait_send()


def hand_over(lo_in, og_in, lo_out, og_out, lo_vmem, og_vmem, sem_in, sem_out):
    def parts(lo, og):
        rows = [pl.ds(k * 128, 128) for k in range(3)]
        return [lo.at[r, :] for r in rows] + [og]

    held = parts(lo_vmem, og_vmem)
    into = [
        pltpu.make_async_copy(a, b, sem_in.at[k])
        for k, (a, b) in enumerate(zip(parts(lo_in, og_in), held))
    ]
    back = [
        pltpu.make_async_copy(a, b, sem_out.at[k])
        for k, (a, b) in enumerate(zip(held, parts(lo_out, og_out)))
    ]
    for copy in into:
        copy.start()
    for a, b in zip(into, back):
        a.wait()
        b.start()
    for copy in back:
        copy.wait()


def per_device(
    patches,
    segment_ids,
    regroup_plan,
    input_weight,
    input_bias,
    skip_weight,
    hidden_weight,
    output_bias,
    norm_gain,
    head_scale,
    qkv_weight,
    out_weight,
    cotangent,
):
    vmem = pl.BlockSpec(memory_space=pltpu.VMEM)
    hbm = pl.BlockSpec(memory_space=pltpu.HBM)
    dma = pltpu.SemaphoreType.DMA
    scratch = [
        pltpu.VMEM((1, WIN), jnp.int32),
        pltpu.VMEM((5, 1, 64), jnp.int32),
        pltpu.VMEM((PATCH, D), BF),
        pltpu.VMEM((D,), F32),
        pltpu.VMEM((PATCH, D), BF),
        pltpu.VMEM((D,), F32),
        pltpu.VMEM((D,), F32),
        pltpu.SMEM((SEQ,), F32),
        pltpu.VMEM((COLS, HW), BF),
        pltpu.VMEM((D + SEQ * PATCH, D), BF),
        pltpu.VMEM((3, D, 2 * LANES), BF),
        pltpu.VMEM((ROWS, D), BF),
        pltpu.VMEM((3, D, LANES), F32),
        pltpu.VMEM((2, HW, ROWS), BF),
        pltpu.VMEM((SEQ * PATCH, ROWS), BF),
        pltpu.VMEM((SEQ * PATCH, D), BF),
        pltpu.VMEM((D, 6 * LANES), BF),
        pltpu.VMEM((WIN, 3 * LANES), BF),
        pltpu.VMEM((4, ROWS, 3 * LANES), BF),
        pltpu.VMEM((4, ROWS, D), BF),
        pltpu.VMEM((8, HW), F32),
        pltpu.VMEM((ZN * 8, HW), F32),
        pltpu.VMEM((XN, 48, HW), BF),
        pltpu.VMEM((D, HW), BF),
        pltpu.VMEM((5, D, LANES), F32),
        pltpu.VMEM((5, 64, LANES), F32),
        pltpu.VMEM((SEQ, HD, ROWS), BF),
        pltpu.VMEM((2, HW, ROWS), BF),
        pltpu.VMEM((HW, HW), F32),
        pltpu.VMEM((HW, ROWS), BF),
        pltpu.VMEM((YN, 160, ROWS), BF),
        pltpu.VMEM((YN, 160, ROWS), BF),
        pltpu.VMEM((XN, YN, 48, HW - ROWS), BF),
        pltpu.VMEM((XN, YN, 48, HW - ROWS), BF),
        pltpu.VMEM((XN, 48, ROWS), BF),
        pltpu.VMEM((XN, 48, ROWS), BF),
        pltpu.VMEM((YN, 48, HW - ROWS), BF),
        pltpu.VMEM((YN, 48, HW - ROWS), BF),
        pltpu.VMEM((GROUP, HW), F32),
        pltpu.VMEM((ZN, 32, LANES), F32),
        pltpu.VMEM((ZN, 32, LANES), BF),
        pltpu.VMEM((ZN, 32, LANES), BF),
        dma((13,)),
        dma((8,)),
        dma((8,)),
        dma((8,)),
        dma((8,)),
        dma((4,)),
        dma((4,)),
        dma((4,)),
        dma((4,)),
        dma((4,)),
        dma((4,)),
        dma((4,)),
        dma((4,)),
        dma((8,)),
        dma((8,)),
        dma((8,)),
        dma((8,)),
        dma((1,)),
        dma((1,)),
        dma((4,)),
        dma((4,)),
        dma((16,)),
        dma((16,)),
        dma((4,)),
        dma((4,)),
        dma((4,)),
        dma((4,)),
        dma((8,)),
        dma((8,)),
    ]
    layer_out, grad = pl.pallas_call(
        whole_layer,
        out_shape=(
            jax.ShapeDtypeStruct((ROWS, D), BF),
            jax.ShapeDtypeStruct((COLS, HW), F32),
        ),
        in_specs=[hbm] * 13,
        out_specs=(vmem, vmem),
        scratch_shapes=scratch,
        compiler_params=pltpu.CompilerParams(
            collective_id=0, has_side_effects=True, vmem_limit_bytes=63 * 1024 * 1024
        ),
        name="whole_layer",
    )(
        patches,
        segment_ids,
        jnp.transpose(regroup_plan, (1, 0, 2)),
        input_weight,
        input_bias,
        skip_weight,
        hidden_weight,
        output_bias,
        norm_gain,
        head_scale,
        jnp.transpose(qkv_weight, (1, 0, 2)),
        jnp.transpose(out_weight),
        cotangent,
    )
    layer_out, grad = pl.pallas_call(
        hand_over,
        out_shape=(
            jax.ShapeDtypeStruct((ROWS, D), BF),
            jax.ShapeDtypeStruct((COLS, HW), F32),
        ),
        in_specs=[hbm, hbm],
        out_specs=(hbm, hbm),
        scratch_shapes=[
            pltpu.VMEM((ROWS, D), BF),
            pltpu.VMEM((COLS, HW), F32),
            dma((4,)),
            dma((4,)),
        ],
        name="hand_over",
    )(layer_out, grad)
    return layer_out, jnp.transpose(grad)


def solution(mesh):
    placed = (
        P(None, ("dp", "seq")),
        P("dp", None),
        P("dp", None, None),
        P(),
        P(),
        P(),
        P(),
        P(),
        P(),
        P(),
        P(),
        P(None, ("dp", "seq")),
        P(("dp", "seq"), None),
    )
    return jax.shard_map(
        per_device,
        mesh=mesh,
        in_specs=placed,
        out_specs=(P(("dp", "seq"), None), P(None, ("dp", "seq"))),
        check_vma=False,
    )
```
